256 devices in a mesh: section: 16 (over y_hi, z), space: 16 (over x, y_lo, core).
Axes of the slice: x: 4, y: 4 (y_hi: 2, y_lo: 2; y = y_hi * 2 + y_lo), z: 8, core: 2. Of those that a mesh axis runs over, the one named last changes fastest.
Arguments:
- top_a: bfloat16 [16, 2048, 1536], P('section', 'space'), may hold values from -6 to 6
- top_b: bfloat16 [16, 2048, 1536], P('section', 'space'), may hold values from -6 to 6
- grad_a: bfloat16 [16, 2048, 1536], P('section', 'space'), may hold values from -6 to 6
- grad_b: bfloat16 [16, 2048, 1536], P('section', 'space'), may hold values from -6 to 6
- w_qkv: bfloat16 [16, 1536, 2304], P('section'), may hold values from -0.15625 to 0.15625
- w_out: bfloat16 [16, 768, 1536], P('section'), may hold values from -0.21875 to 0.21875
- kernel: float32 [16, 27, 1536], P('section'), may hold values from -1.75 to 1.75
- tau: float32 [16, 12], P('section'), may hold values from 4 to 20
- block_owner: int32 [16, 2], replicated, may hold values from 0 to 15, as said below
Outputs:
- rebuilt_a: bfloat16 [16, 2048, 1536], P('section', 'space')
- rebuilt_b: bfloat16 [16, 2048, 1536], P('section', 'space')
- passed_a: bfloat16 [16, 2048, 1536], P('section', 'space')
- passed_b: bfloat16 [16, 2048, 1536], P('section', 'space')
The draws below stay inside these ranges and needn't reach their ends.
Inputs may be any that keep to these rules, and one draw needn't show every extreme that they name: `block_owner`: row i lists tile i and one tile beside it, i - 1 or i + 1, in either order; tile 0's other tile is 1 and tile 16 - 1's is 14.
All inputs are finite; a program needn't handle non-finite values.
Results may differ from the reference program's by a relative error of at most 0.039.
Values may be sent and summed in bfloat16 or wider, within the bound.
No kernel may reach another device: no remote copies, remote signals or barrier semaphores. Data moves between devices by JAX's collectives and lax.ppermute only.
A program may use at most 128 MiB of HBM per device.

```python
import math
import jax
import jax.numpy as jnp
from jax import lax

D = 1536
HEADS = 12
HEAD = 64
FT = 4
FW = 16
NB = 2
STEPS = 2
BLOCK = 128
TILES = 16
TOKENS = 2048
SECTIONS = 16


def draw_block_owner(key, part):
    key = jax.random.fold_in(key, 11)
    side_key = jax.random.fold_in(key, 1)
    order_key = jax.random.fold_in(key, 2)
    tile_ids = jnp.arange(TILES, dtype=jnp.int32)
    beside = jax.random.randint(side_key, (TILES,), 0, 2).astype(jnp.int32) * 2 - 1
    beside = jnp.where(tile_ids == 0, 1, jnp.where(tile_ids == TILES - 1, -1, beside))
    other = tile_ids + beside
    flip = jax.random.randint(order_key, (TILES,), 0, 2).astype(jnp.int32)
    first = jnp.where(flip == 1, other, tile_ids)
    second = jnp.where(flip == 1, tile_ids, other)
    return jnp.stack([first, second], axis=1).astype(jnp.int32)


def level_of(rng, extent, shards, least, top_value):
    factor_of = 1.0
    for dim, shards_of in shards:
        draws = jax.random.uniform(jax.random.fold_in(jax.random.fold_in(rng, 6), dim), (shards_of,), jnp.float32, least / len(shards), top_value / len(shards))
        factor_of = factor_of * jnp.repeat(jnp.exp(draws), extent[dim] // shards_of).reshape((-1,) + (1,) * (len(extent) - 1 - dim))
    return factor_of


def noise(own_key, dims, deviation, limit, cuts=(), kind=jnp.bfloat16):
    level = level_of(own_key, dims, cuts, -0.22, 0.18) if cuts else 1.0
    entries = jax.random.normal(own_key, dims, jnp.float32) * deviation * level
    return jnp.minimum(jnp.maximum(entries, -limit), limit).astype(kind)


def setup_inputs(seed: int = 0) -> dict:
    streams_of = jax.random.split(jax.random.key(seed), 10)
    return {
        "top_a": noise(streams_of[0], (SECTIONS, TOKENS, D), 1.0, 6.0, ((0, 16), (1, 16))),
        "top_b": noise(streams_of[1], (SECTIONS, TOKENS, D), 1.0, 6.0, ((0, 16), (1, 16))),
        "grad_a": noise(streams_of[2], (SECTIONS, TOKENS, D), 1.0, 6.0, ((0, 16), (1, 16))),
        "grad_b": noise(streams_of[3], (SECTIONS, TOKENS, D), 1.0, 6.0, ((0, 16), (1, 16))),
        "w_qkv": noise(streams_of[4], (SECTIONS, D, 3 * HEADS * HEAD), D ** -0.5, 0.15625, ((0, 16),)),
        "w_out": noise(streams_of[5], (SECTIONS, HEADS * HEAD, D), (HEADS * HEAD) ** -0.5, 0.21875, ((0, 16),)),
        "kernel": noise(streams_of[6], (SECTIONS, 27, 2 * HEADS * HEAD), 0.3, 1.75, ((0, 16),), jnp.float32),
        "tau": jnp.clip(jnp.exp(math.log(20.0) - 1.609438 * jax.random.uniform(streams_of[7], (SECTIONS, HEADS), jnp.float32) ** level_of(streams_of[7], (SECTIONS, HEADS), ((0, 16),), -0.2, 0.2)), 4.0, 20.0),
        "block_owner": draw_block_owner(jax.random.fold_in(streams_of[9], 71), 0),
    }


EPS_NORM = 1e-05
EPS_HEAD = 1e-06

def rounded(values_in):
    return lax.optimization_barrier(values_in.astype(jnp.bfloat16))

def normalize_rows(features):
    average = lax.optimization_barrier(jnp.mean(features, axis=-1, keepdims=True))
    centred = features - average
    inverse = lax.rsqrt(lax.optimization_barrier(jnp.mean(centred * centred, axis=-1, keepdims=True)) + EPS_NORM)
    return (centred * inverse, inverse)

def normalize_back(normalized, inverse, gradient):
    grad_mean = lax.optimization_barrier(jnp.mean(gradient, axis=-1, keepdims=True))
    cross_mean = lax.optimization_barrier(jnp.mean(gradient * normalized, axis=-1, keepdims=True))
    return inverse * (gradient - grad_mean - normalized * cross_mean)

def head_unit(heads_in):
    inverse = lax.rsqrt(lax.optimization_barrier(jnp.sum(heads_in * heads_in, axis=-1, keepdims=True)) + EPS_HEAD)
    return (heads_in * inverse, inverse)

def head_unit_back(unit_rows, inverse, gradient):
    return inverse * (gradient - unit_rows * lax.optimization_barrier(jnp.sum(unit_rows * gradient, axis=-1, keepdims=True)))

def pool_core(extended, kernel, direction):
    row_count = extended.shape[0] - 2
    padded = jnp.pad(extended, ((0, 0), (1, 1), (1, 1), (0, 0)))
    summed = jnp.zeros((row_count, FT, FW, extended.shape[3]), jnp.float32)
    for off_row in range(3):
        for off_frame in range(3):
            for off_col in range(3):
                tap_weight = kernel[off_row * 9 + off_frame * 3 + off_col]
                start_row = 1 + direction * (off_row - 1)
                start_frame = 1 + direction * (off_frame - 1)
                start_col = 1 + direction * (off_col - 1)
                window = padded[start_row:start_row + row_count, start_frame:start_frame + FT, start_col:start_col + FW]
                summed = summed + tap_weight * window.astype(jnp.float32)
    return summed

def layer_back(carried, w_qkv, w_out, kernel, head_scale, block_owner):
    top_a, top_b, grad_a, grad_b = carried
    token_count = top_a.shape[0]
    tile_count = token_count // BLOCK
    row_count = token_count // (FT * FW)
    hidden = HEADS * HEAD
    normalized, inverse = normalize_rows(top_a.astype(jnp.float32))
    projected = rounded(jnp.dot(rounded(normalized), w_qkv, preferred_element_type=jnp.float32))
    queries = projected[:, :hidden]
    raw_kv = projected[:, hidden:].reshape(row_count, FT, FW, 2 * hidden)
    extended = jnp.pad(raw_kv, ((1, 1), (0, 0), (0, 0), (0, 0)))
    pooled = rounded(pool_core(extended, kernel, 1)).reshape(token_count, 2 * hidden)
    q_unit, q_inverse = head_unit(queries.astype(jnp.float32).reshape(token_count, HEADS, HEAD))
    k_unit, k_inverse = head_unit(pooled[:, :hidden].astype(jnp.float32).reshape(token_count, HEADS, HEAD))
    q_tiles = rounded(q_unit).reshape(tile_count, BLOCK, HEADS, HEAD)
    k_tiles = rounded(k_unit).reshape(tile_count, BLOCK, HEADS, HEAD)
    v_tiles = pooled[:, hidden:].reshape(tile_count, BLOCK, HEADS, HEAD)
    grad_out = rounded(jnp.dot(grad_b, w_out.T, preferred_element_type=jnp.float32))
    g_tiles = grad_out.reshape(tile_count, BLOCK, HEADS, HEAD)
    scale_col = head_scale[:, None, None]

    def per_tile(tile_index):
        owners = block_owner[tile_index]
        key_rows = k_tiles[owners].reshape(NB * BLOCK, HEADS, HEAD).astype(jnp.float32)
        value_rows = v_tiles[owners].reshape(NB * BLOCK, HEADS, HEAD).astype(jnp.float32)
        q_low = q_tiles[tile_index].astype(jnp.float32)
        gradient = g_tiles[tile_index].astype(jnp.float32)
        scores = jnp.einsum('qhe,khe->hqk', q_low, key_rows) * scale_col
        exponent = jnp.exp(scores)
        attn_probs = exponent / lax.optimization_barrier(jnp.sum(exponent, axis=-1, keepdims=True))
        probs_low = rounded(attn_probs).astype(jnp.float32)
        output = jnp.einsum('hqk,khe->qhe', probs_low, value_rows)
        grad_probs = jnp.einsum('qhe,khe->hqk', gradient, value_rows)
        deltas = lax.optimization_barrier(jnp.sum(attn_probs * grad_probs, axis=-1, keepdims=True))
        grad_scores = rounded(attn_probs * (grad_probs - deltas) * scale_col).astype(jnp.float32)
        grad_q = jnp.einsum('hqk,khe->qhe', grad_scores, key_rows)
        grad_k = jnp.einsum('hqk,qhe->khe', grad_scores, q_low)
        grad_v = jnp.einsum('hqk,qhe->khe', probs_low, gradient)
        key_part = jnp.concatenate([grad_k.reshape(NB, BLOCK, hidden), grad_v.reshape(NB, BLOCK, hidden)], axis=-1)
        return (rounded(output), grad_q, rounded(key_part))
    attended, grad_q, key_part = lax.map(per_tile, jnp.arange(tile_count, dtype=jnp.int32))
    branch = jnp.dot(attended.reshape(token_count, hidden), w_out, preferred_element_type=jnp.float32)
    rebuilt = (top_b.astype(jnp.float32) - branch).astype(jnp.bfloat16)
    key_sum = jax.ops.segment_sum(key_part.astype(jnp.float32).reshape(tile_count * NB, BLOCK, 2 * hidden), block_owner.reshape(-1), num_segments=tile_count)
    key_sum = key_sum.reshape(token_count, 2 * hidden)
    grad_keys = head_unit_back(k_unit, k_inverse, key_sum[:, :hidden].reshape(token_count, HEADS, HEAD)).reshape(token_count, hidden)
    grad_pooled = rounded(jnp.concatenate([grad_keys, key_sum[:, hidden:]], axis=1)).reshape(row_count, FT, FW, 2 * hidden)
    grad_raw = pool_core(jnp.pad(grad_pooled, ((1, 1), (0, 0), (0, 0), (0, 0))), kernel, -1).reshape(token_count, 2 * hidden)
    grad_query = head_unit_back(q_unit, q_inverse, grad_q.reshape(token_count, HEADS, HEAD)).reshape(token_count, hidden)
    grad_proj = rounded(jnp.concatenate([grad_query, grad_raw], axis=1))
    grad_normed = jnp.dot(grad_proj, w_qkv.T, preferred_element_type=jnp.float32)
    new_grad = (grad_a.astype(jnp.float32) + normalize_back(normalized, inverse, grad_normed)).astype(jnp.bfloat16)
    return (rebuilt, top_a, grad_b, new_grad)

def reference(top_a, top_b, grad_a, grad_b, w_qkv, w_out, kernel, tau, block_owner):
    carried = (top_a, top_b, grad_a, grad_b)

    def per_section(section_item):
        return layer_back(section_item[:4], section_item[4], section_item[5], section_item[6], section_item[7], block_owner)
    for layer_step in range(STEPS):
        carried = lax.map(per_section, carried + (w_qkv, w_out, kernel, tau))
        carried = tuple((jnp.roll(member, -1, axis=0) for member in carried))
    return (carried[0], carried[1], carried[2], carried[3])
```

```python
import functools

import jax
import jax.numpy as jnp
from jax import lax
from jax.experimental import pallas as pl
from jax.experimental.pallas import tpu as pltpu
from jax.sharding import PartitionSpec as P

HEADS = 12
HEAD = 64
FT = 4
FW = 16
STEPS = 2
PAIRS = HEADS // 2
PW = 2 * HEAD
ROW = FT * FW

EPS_NORM = 1e-05
EPS_HEAD = 1e-06

F32 = jnp.float32
BF16 = jnp.bfloat16
VMEM = pltpu.VMEM
SMEM = pltpu.SMEM


def dot(a, b):
    return jnp.dot(a, b, preferred_element_type=F32)


def dot_nt(a, b):
    return lax.dot_general(a, b, (((1,), (1,)), ((), ())), preferred_element_type=F32)


def normalize_rows(features):
    average = jnp.mean(features, axis=-1, keepdims=True)
    centred = features - average
    inverse = lax.rsqrt(jnp.mean(centred * centred, axis=-1, keepdims=True) + EPS_NORM)
    return centred * inverse, inverse


def first_half(shape):
    return lax.broadcasted_iota(jnp.int32, shape, 1) < HEAD


def pair_sums(values, first):
    low = jnp.sum(jnp.where(first, values, 0.0), axis=-1, keepdims=True)
    high = jnp.sum(jnp.where(first, 0.0, values), axis=-1, keepdims=True)
    return jnp.where(first, low, high)


def pair_unit(values, first):
    inverse = lax.rsqrt(pair_sums(values * values, first) + EPS_HEAD)
    return values * inverse, inverse


def pair_unit_back(unit, inverse, gradient, first):
    return inverse * (gradient - unit * pair_sums(unit * gradient, first))


def pool_lanes(ext_ref, taps, flip):
    column = lax.broadcasted_iota(jnp.int32, (FW, 128), 0)
    blocks = []
    for row in range(2):
        for frame in range(FT):
            parts = [None, None, None]
            for dr in range(3):
                for df in range(3):
                    source = frame + df - 1
                    if source < 0 or source >= FT:
                        continue
                    start = (row + dr) * ROW + source * FW
                    block = ext_ref[start : start + FW, :]
                    for dc in range(3):
                        tap = dr * 9 + df * 3 + dc
                        term = taps[26 - tap if flip else tap] * block
                        parts[dc] = term if parts[dc] is None else parts[dc] + term
            left = jnp.where(column == 0, 0.0, pltpu.roll(parts[0], 1, 0))
            right = jnp.where(column == FW - 1, 0.0, pltpu.roll(parts[2], FW - 1, 0))
            blocks.append(parts[1] + left + right)
    return jnp.concatenate(blocks, axis=0)


def load_taps(kern_ref, lanes):
    return [jnp.broadcast_to(kern_ref[t : t + 1, lanes], (FW, 128)) for t in range(27)]


def project_kernel(a_ref, w_ref, out_ref):
    normalized, _ = normalize_rows(a_ref[...].astype(F32))
    low = normalized.astype(BF16)
    for c in range(0, w_ref.shape[1], 256):
        out_ref[:, c : c + 256] = dot(low, w_ref[:, c : c + 256]).astype(BF16)


def pool_kernel(prev_ref, next_ref, w_ref, proj_ref, kern_ref, kv_ref, pk_ref, ext_ref):
    hidden = pk_ref.shape[1]
    halo = jnp.concatenate([prev_ref[...], next_ref[...]], axis=0).astype(F32)
    low = normalize_rows(halo)[0].astype(BF16)
    first = first_half((128, 128))
    for c in range(0, 2 * hidden, 256):
        outer = dot(low, w_ref[:, hidden + c : hidden + c + 256]).astype(BF16).astype(F32)
        for j in (0, 128):
            at = c + j
            ext_ref[0:ROW, :] = outer[:ROW, j : j + 128]
            ext_ref[ROW : ROW + 128, :] = proj_ref[:, hidden + at : hidden + at + 128].astype(F32)
            ext_ref[ROW + 128 :, :] = outer[ROW:, j : j + 128]
            pooled = pool_lanes(ext_ref, load_taps(kern_ref, slice(at, at + 128)), False).astype(BF16)
            if at < hidden:
                pk_ref[:, at : at + 128] = pooled
                kv_ref[:, at : at + 128] = pair_unit(pooled.astype(F32), first)[0].astype(BF16)
            else:
                kv_ref[:, at : at + 128] = pooled


def attention_kernel(
    flags_ref, tau_ref, proj_ref, own_ref, prev_ref, next_ref, gb_ref, wout_ref,
    att_ref, gq_ref, part_own_ref, part_near_ref,
):
    hidden = att_ref.shape[1]
    from_prev = flags_ref[0] == 1
    first = first_half((128, 128))
    first_low = first_half((256, 128))
    gb = gb_ref[...]

    def both(at):
        near = jnp.where(from_prev, prev_ref[:, at : at + PW], next_ref[:, at : at + PW])
        return jnp.concatenate([own_ref[:, at : at + PW], near], axis=0)

    def masked(rows):
        zero = jnp.zeros_like(rows)
        return jnp.concatenate(
            [jnp.where(first_low, rows, zero), jnp.where(first_low, zero, rows)], axis=0
        )

    for p in range(PAIRS):
        at = p * PW
        g2 = dot_nt(gb, wout_ref[at : at + PW, :]).astype(BF16)
        q_unit, q_inverse = pair_unit(proj_ref[:, at : at + PW].astype(F32), first)
        q_low = q_unit.astype(BF16)
        keys = masked(both(at))
        values = masked(both(hidden + at))
        scores = dot_nt(q_low, keys)
        grad_probs = dot_nt(g2, values)
        probs, grads = [], []
        for half in range(2):
            scale = tau_ref[2 * p + half]
            cut = slice(half * 256, half * 256 + 256)
            exponent = jnp.exp(scores[:, cut] * scale)
            prob = exponent * (1.0 / jnp.sum(exponent, axis=-1, keepdims=True))
            gp = grad_probs[:, cut]
            delta = jnp.sum(prob * gp, axis=-1, keepdims=True)
            probs.append(prob.astype(BF16))
            grads.append((scale * prob * (gp - delta)).astype(BF16))
        prob_low = jnp.concatenate(probs, axis=1)
        grad_scores = jnp.concatenate(grads, axis=1)
        att_ref[:, at : at + PW] = dot(prob_low, values).astype(BF16)
        grad_q = dot(grad_scores, keys)
        gq_ref[:, at : at + PW] = pair_unit_back(q_unit, q_inverse, grad_q, first).astype(BF16)
        grad_k = dot(grad_scores.T, q_low)
        grad_v = dot(prob_low.T, g2)
        grad_k = jnp.where(first_low, grad_k[:256], grad_k[256:]).astype(BF16)
        grad_v = jnp.where(first_low, grad_v[:256], grad_v[256:]).astype(BF16)
        part_own_ref[:, at : at + PW] = grad_k[:128]
        part_near_ref[:, at : at + PW] = grad_k[128:]
        part_own_ref[:, hidden + at : hidden + at + PW] = grad_v[:128]
        part_near_ref[:, hidden + at : hidden + at + PW] = grad_v[128:]


def output_kernel(att_ref, wout_ref, b_ref, out_ref):
    att = att_ref[...]
    for c in range(0, out_ref.shape[1], 256):
        cut = slice(c, c + 256)
        out_ref[:, cut] = (b_ref[:, cut].astype(F32) - dot(att, wout_ref[:, cut])).astype(BF16)


def key_kernel(flags_ref, own_ref, prev_ref, next_ref, pk_ref, out_ref):
    hidden = pk_ref.shape[1]
    first = first_half((128, 128))
    use_prev = flags_ref[1] == 1
    use_next = flags_ref[2] == 1
    for at in range(0, 2 * hidden, 128):
        cut = slice(at, at + 128)
        total = own_ref[:, cut].astype(F32)
        total = total + jnp.where(use_prev, prev_ref[:, cut].astype(F32), 0.0)
        total = total + jnp.where(use_next, next_ref[:, cut].astype(F32), 0.0)
        if at < hidden:
            unit, inverse = pair_unit(pk_ref[:, cut].astype(F32), first)
            total = pair_unit_back(unit, inverse, total, first)
        out_ref[:, cut] = total.astype(BF16)


def final_kernel(
    prev_ref, own_ref, next_ref, gq_ref, w_ref, kern_ref, a_ref, ga_ref, out_ref, ext_ref, gp_ref, acc_ref
):
    hidden = gq_ref.shape[1]
    width = a_ref.shape[1]
    gp_ref[:, :hidden] = gq_ref[...]
    for at in range(0, 2 * hidden, 128):
        cut = slice(at, at + 128)
        ext_ref[0:ROW, :] = prev_ref[:, cut].astype(F32)
        ext_ref[ROW : ROW + 128, :] = own_ref[:, cut].astype(F32)
        ext_ref[ROW + 128 :, :] = next_ref[:, cut].astype(F32)
        pooled = pool_lanes(ext_ref, load_taps(kern_ref, cut), True)
        gp_ref[:, hidden + at : hidden + at + 128] = pooled.astype(BF16)
    grad_proj = gp_ref[...]
    for c in range(0, width, 256):
        acc_ref[:, c : c + 256] = dot_nt(grad_proj, w_ref[c : c + 256, :])
    normalized, inverse = normalize_rows(a_ref[...].astype(F32))
    grad = acc_ref[...]
    grad_mean = jnp.mean(grad, axis=-1, keepdims=True)
    cross_mean = jnp.mean(grad * normalized, axis=-1, keepdims=True)
    back = inverse * (grad - grad_mean - normalized * cross_mean)
    out_ref[...] = (ga_ref[...].astype(F32) + back).astype(BF16)


def call(kernel, name, outs, specs, flops, scratch=()):
    def run(*args):
        moved = sum(x.size * x.dtype.itemsize for x in args)
        return pl.pallas_call(
            kernel,
            name=name,
            out_shape=[jax.ShapeDtypeStruct(s, BF16) for s in outs],
            in_specs=[pl.BlockSpec(memory_space=s) for s in specs],
            out_specs=[pl.BlockSpec(memory_space=VMEM) for _ in outs],
            scratch_shapes=list(scratch),
            compiler_params=pltpu.CompilerParams(vmem_limit_bytes=40 * 1024 * 1024),
            cost_estimate=pl.CostEstimate(flops=flops, bytes_accessed=moved, transcendentals=0),
        )(*args)

    return run


def pass_on(value, by):
    count = lax.axis_size("space")
    pairs = [(i, i + by) for i in range(count) if 0 <= i + by < count]
    return lax.ppermute(value, "space", pairs)


def shift(value):
    count = lax.axis_size("section")
    return lax.ppermute(value, "section", [(i, (i - 1) % count) for i in range(count)])


def layer(state, w_qkv, w_out, kern, tau, flags):
    a, b, ga, gb = state
    block, width = a.shape
    hidden = w_out.shape[0]
    a_prev = pass_on(a[block - ROW :], 1)
    a_next = pass_on(a[:ROW], -1)
    (proj,) = call(
        project_kernel, "project", [(block, 3 * hidden)], [VMEM] * 2, 2 * block * width * 3 * hidden
    )(a, w_qkv)
    kv, pk = call(
        pool_kernel, "pool", [(block, 2 * hidden), (block, hidden)], [VMEM] * 5,
        2 * block * width * 2 * hidden, [pltpu.VMEM((256, 128), F32)],
    )(a_prev, a_next, w_qkv, proj, kern)
    kv_prev = pass_on(kv, 1)
    kv_next = pass_on(kv, -1)
    att, gq, part_own, part_near = call(
        attention_kernel, "attention",
        [(block, hidden), (block, hidden), (block, 2 * hidden), (block, 2 * hidden)],
        [SMEM] * 2 + [VMEM] * 6, 2 * block * width * hidden * 3,
    )(flags, tau, proj, kv, kv_prev, kv_next, gb, w_out)
    part_prev = pass_on(part_near, 1)
    part_next = pass_on(part_near, -1)
    (rebuilt,) = call(
        output_kernel, "output", [(block, width)], [VMEM] * 3, 2 * block * width * hidden
    )(att, w_out, b)
    (gpool,) = call(key_kernel, "keys", [(block, 2 * hidden)], [SMEM] + [VMEM] * 4, block * width * 40)(
        flags, part_own, part_prev, part_next, pk
    )
    g_prev = pass_on(gpool[block - ROW :], 1)
    g_next = pass_on(gpool[:ROW], -1)
    (new_grad,) = call(
        final_kernel, "final", [(block, width)], [VMEM] * 8, 2 * block * width * 3 * hidden,
        [
            pltpu.VMEM((256, 128), F32),
            pltpu.VMEM((block, 3 * hidden), BF16),
            pltpu.VMEM((block, width), F32),
        ],
    )(g_prev, gpool, g_next, gq, w_qkv, kern, a, ga)
    return rebuilt, a, gb, new_grad


def tile_flags(block_owner):
    tile = lax.axis_index("space")
    count = lax.axis_size("space")
    ids = jnp.arange(count, dtype=jnp.int32)
    lists_prev = jnp.any(block_owner == (ids - 1)[:, None], axis=1).astype(jnp.int32)
    lists_next = jnp.any(block_owner == (ids + 1)[:, None], axis=1).astype(jnp.int32)
    take = lambda v, i: jnp.sum(jnp.where(ids == i, v, 0))
    return jnp.stack([take(lists_prev, tile), take(lists_next, tile - 1), take(lists_prev, tile + 1)])


def body(top_a, top_b, grad_a, grad_b, w_qkv, w_out, kernel, tau, block_owner):
    flags = tile_flags(block_owner)
    state = (top_a[0], top_b[0], grad_a[0], grad_b[0])
    for _ in range(STEPS):
        result = layer(state, w_qkv[0], w_out[0], kernel[0], tau[0], flags)
        state = tuple(shift(member) for member in result)
    return tuple(member[None] for member in state)


def solution(mesh):
    state = P("section", "space", None)
    weights = P("section", None, None)
    return jax.shard_map(
        body,
        mesh=mesh,
        in_specs=(state,) * 4 + (weights,) * 3 + (P("section", None), P()),
        out_specs=(state,) * 4,
        check_vma=False,
    )
```

```python
import functools

import jax
import jax.numpy as jnp
from jax import lax
from jax.experimental import pallas as pl
from jax.experimental.pallas import tpu as pltpu
from jax.sharding import PartitionSpec as P

HEADS = 12
HEAD = 64
FT = 4
FW = 16
PAIRS = HEADS // 2
PW = 2 * HEAD
ROW = FT * FW

EPS_NORM = 1e-05
EPS_HEAD = 1e-06

F32 = jnp.float32
BF16 = jnp.bfloat16
VMEM = pltpu.VMEM
SMEM = pltpu.SMEM


def dot(a, b):
    return jnp.dot(a, b, preferred_element_type=F32)


def dot_nt(a, b):
    return lax.dot_general(a, b, (((1,), (1,)), ((), ())), preferred_element_type=F32)


def normalize_rows(features):
    average = jnp.mean(features, axis=-1, keepdims=True)
    centred = features - average
    inverse = lax.rsqrt(jnp.mean(centred * centred, axis=-1, keepdims=True) + EPS_NORM)
    return centred * inverse, inverse


def first_half(shape):
    return lax.broadcasted_iota(jnp.int32, shape, 1) < HEAD


def pair_sums(values, first):
    low = jnp.sum(jnp.where(first, values, 0.0), axis=-1, keepdims=True)
    high = jnp.sum(jnp.where(first, 0.0, values), axis=-1, keepdims=True)
    return jnp.where(first, low, high)


def pair_unit(values, first):
    inverse = lax.rsqrt(pair_sums(values * values, first) + EPS_HEAD)
    return values * inverse, inverse


def pair_unit_back(unit, inverse, gradient, first):
    return inverse * (gradient - unit * pair_sums(unit * gradient, first))


def pool_lanes(ext_ref, taps, flip):
    column = lax.broadcasted_iota(jnp.int32, (FW, 128), 0)
    blocks = []
    for row in range(2):
        for frame in range(FT):
            parts = [None, None, None]
            for dr in range(3):
                for df in range(3):
                    source = frame + df - 1
                    if source < 0 or source >= FT:
                        continue
                    start = (row + dr) * ROW + source * FW
                    block = ext_ref[start : start + FW, :]
                    for dc in range(3):
                        tap = dr * 9 + df * 3 + dc
                        term = taps[26 - tap if flip else tap] * block
                        parts[dc] = term if parts[dc] is None else parts[dc] + term
            left = jnp.where(column == 0, 0.0, pltpu.roll(parts[0], 1, 0))
            right = jnp.where(column == FW - 1, 0.0, pltpu.roll(parts[2], FW - 1, 0))
            blocks.append(parts[1] + left + right)
    return jnp.concatenate(blocks, axis=0)


def load_taps(kern_ref, lanes):
    return [jnp.broadcast_to(kern_ref[t : t + 1, lanes], (FW, 128)) for t in range(27)]


def project_kernel(a_ref, w_ref, out_ref):
    normalized, _ = normalize_rows(a_ref[...].astype(F32))
    low = normalized.astype(BF16)
    for c in range(0, w_ref.shape[1], 256):
        out_ref[:, c : c + 256] = dot(low, w_ref[:, c : c + 256]).astype(BF16)


def pool_kernel(flags_ref, cross_ref, inner_ref, w_ref, proj_ref, kern_ref, kv_ref, pk_ref, ext_ref):
    hidden = pk_ref.shape[1]
    odd = flags_ref[3] == 1
    cross, inner = cross_ref[...], inner_ref[...]
    halo = jnp.concatenate(
        [jnp.where(odd, inner, cross), jnp.where(odd, cross, inner)], axis=0
    ).astype(F32)
    low = normalize_rows(halo)[0].astype(BF16)
    first = first_half((128, 128))
    for c in range(0, 2 * hidden, 256):
        outer = dot(low, w_ref[:, hidden + c : hidden + c + 256]).astype(BF16).astype(F32)
        for j in (0, 128):
            at = c + j
            ext_ref[0:ROW, :] = outer[:ROW, j : j + 128]
            ext_ref[ROW : ROW + 128, :] = proj_ref[:, hidden + at : hidden + at + 128].astype(F32)
            ext_ref[ROW + 128 :, :] = outer[ROW:, j : j + 128]
            pooled = pool_lanes(ext_ref, load_taps(kern_ref, slice(at, at + 128)), False).astype(BF16)
            if at < hidden:
                pk_ref[:, at : at + 128] = pooled
                kv_ref[:, at : at + 128] = pair_unit(pooled.astype(F32), first)[0].astype(BF16)
            else:
                kv_ref[:, at : at + 128] = pooled


def attention_kernel(
    flags_ref, tau_ref, proj_ref, own_ref, cross_ref, inner_ref, gb_ref, wout_ref,
    att_ref, gq_ref, part_own_ref, part_near_ref,
):
    hidden = att_ref.shape[1]
    from_cross = flags_ref[0] == 1
    first = first_half((128, 128))
    first_low = first_half((256, 128))
    gb = gb_ref[...]

    def both(at):
        near = jnp.where(from_cross, cross_ref[:, at : at + PW], inner_ref[:, at : at + PW])
        return jnp.concatenate([own_ref[:, at : at + PW], near], axis=0)

    def masked(rows):
        zero = jnp.zeros_like(rows)
        return jnp.concatenate(
            [jnp.where(first_low, rows, zero), jnp.where(first_low, zero, rows)], axis=0
        )

    for p in range(PAIRS):
        at = p * PW
        g2 = dot_nt(gb, wout_ref[at : at + PW, :]).astype(BF16)
        q_unit, q_inverse = pair_unit(proj_ref[:, at : at + PW].astype(F32), first)
        q_low = q_unit.astype(BF16)
        keys = masked(both(at))
        values = masked(both(hidden + at))
        scores = dot_nt(q_low, keys)
        grad_probs = dot_nt(g2, values)
        probs, grads = [], []
        for half in range(2):
            scale = tau_ref[2 * p + half]
            cut = slice(half * 256, half * 256 + 256)
            exponent = jnp.exp(scores[:, cut] * scale)
            prob = exponent * (1.0 / jnp.sum(exponent, axis=-1, keepdims=True))
            gp = grad_probs[:, cut]
            delta = jnp.sum(prob * gp, axis=-1, keepdims=True)
            probs.append(prob.astype(BF16))
            grads.append((scale * prob * (gp - delta)).astype(BF16))
        prob_low = jnp.concatenate(probs, axis=1)
        grad_scores = jnp.concatenate(grads, axis=1)
        att_ref[:, at : at + PW] = dot(prob_low, values).astype(BF16)
        grad_q = dot(grad_scores, keys)
        gq_ref[:, at : at + PW] = pair_unit_back(q_unit, q_inverse, grad_q, first).astype(BF16)
        grad_k = dot(grad_scores.T, q_low)
        grad_v = dot(prob_low.T, g2)
        grad_k = jnp.where(first_low, grad_k[:256], grad_k[256:]).astype(BF16)
        grad_v = jnp.where(first_low, grad_v[:256], grad_v[256:]).astype(BF16)
        part_own_ref[:, at : at + PW] = grad_k[:128]
        part_near_ref[:, at : at + PW] = grad_k[128:]
        part_own_ref[:, hidden + at : hidden + at + PW] = grad_v[:128]
        part_near_ref[:, hidden + at : hidden + at + PW] = grad_v[128:]


def output_kernel(att_ref, wout_ref, b_ref, out_ref):
    att = att_ref[...]
    for c in range(0, out_ref.shape[1], 256):
        cut = slice(c, c + 256)
        out_ref[:, cut] = (b_ref[:, cut].astype(F32) - dot(att, wout_ref[:, cut])).astype(BF16)


def key_kernel(flags_ref, own_ref, cross_ref, inner_ref, pk_ref, out_ref, cross_out_ref, inner_out_ref):
    hidden = pk_ref.shape[1]
    first = first_half((128, 128))
    use_cross = flags_ref[1] == 1
    use_inner = flags_ref[2] == 1
    odd = flags_ref[3] == 1
    for at in range(0, 2 * hidden, 128):
        cut = slice(at, at + 128)
        total = own_ref[:, cut].astype(F32)
        total = total + jnp.where(use_cross, cross_ref[:, cut].astype(F32), 0.0)
        total = total + jnp.where(use_inner, inner_ref[:, cut].astype(F32), 0.0)
        if at < hidden:
            unit, inverse = pair_unit(pk_ref[:, cut].astype(F32), first)
            total = pair_unit_back(unit, inverse, total, first)
        total = total.astype(BF16)
        out_ref[:, cut] = total
        cross_out_ref[:, cut] = jnp.where(odd, total[ROW:], total[:ROW])
        inner_out_ref[:, cut] = jnp.where(odd, total[:ROW], total[ROW:])


def final_kernel(
    flags_ref, cross_ref, own_ref, inner_ref, gq_ref, w_ref, kern_ref, a_ref, ga_ref,
    out_ref, ext_ref, gp_ref, acc_ref,
):
    odd = flags_ref[3] == 1
    hidden = gq_ref.shape[1]
    width = a_ref.shape[1]
    gp_ref[:, :hidden] = gq_ref[...]
    for at in range(0, 2 * hidden, 128):
        cut = slice(at, at + 128)
        cross, inner = cross_ref[:, cut], inner_ref[:, cut]
        ext_ref[0:ROW, :] = jnp.where(odd, inner, cross).astype(F32)
        ext_ref[ROW : ROW + 128, :] = own_ref[:, cut].astype(F32)
        ext_ref[ROW + 128 :, :] = jnp.where(odd, cross, inner).astype(F32)
        pooled = pool_lanes(ext_ref, load_taps(kern_ref, cut), True)
        gp_ref[:, hidden + at : hidden + at + 128] = pooled.astype(BF16)
    grad_proj = gp_ref[...]
    for c in range(0, width, 256):
        acc_ref[:, c : c + 256] = dot_nt(grad_proj, w_ref[c : c + 256, :])
    normalized, inverse = normalize_rows(a_ref[...].astype(F32))
    grad = acc_ref[...]
    grad_mean = jnp.mean(grad, axis=-1, keepdims=True)
    cross_mean = jnp.mean(grad * normalized, axis=-1, keepdims=True)
    back = inverse * (grad - grad_mean - normalized * cross_mean)
    out_ref[...] = (ga_ref[...].astype(F32) + back).astype(BF16)


def call(kernel, name, outs, specs, flops, scratch=()):
    def run(*args):
        moved = sum(x.size * x.dtype.itemsize for x in args)
        return pl.pallas_call(
            kernel,
            name=name,
            out_shape=[jax.ShapeDtypeStruct(s, BF16) for s in outs],
            in_specs=[pl.BlockSpec(memory_space=s) for s in specs],
            out_specs=[pl.BlockSpec(memory_space=VMEM) for _ in outs],
            scratch_shapes=list(scratch),
            compiler_params=pltpu.CompilerParams(vmem_limit_bytes=40 * 1024 * 1024),
            cost_estimate=pl.CostEstimate(flops=flops, bytes_accessed=moved, transcendentals=0),
        )(*args)

    return run


SECTIONS = 16
TILES = 16


def start_layout(section, x):
    return 0


def first_layout(section, x):
    return 0


def second_layout(section, x):
    return 1 if section in (7, 15) else 0


def place(layout, section, tile):
    return section * TILES + (tile ^ (2 * layout(section, tile // 4)))


AXES = ("section", "space")


def move(value, source, target, by):
    pairs = [
        (place(source, s, t), place(target, (s + by) % SECTIONS, t))
        for s in range(SECTIONS)
        for t in range(TILES)
    ]
    return lax.ppermute(value, AXES, pairs)


def swap_cross(value, layout):
    pairs = []
    for s in range(SECTIONS):
        for t in range(1, TILES - 1, 2):
            one, two = place(layout, s, t), place(layout, s, t + 1)
            pairs += [(one, two), (two, one)]
    return lax.ppermute(value, AXES, pairs)


def swap_inner(value, layout):
    pairs = []
    for s in range(SECTIONS):
        for t in range(0, TILES, 2):
            one, two = place(layout, s, t), place(layout, s, t + 1)
            pairs += [(one, two), (two, one)]
    return lax.ppermute(value, AXES, pairs)


def exchange(cross, inner, layout):
    return swap_cross(cross, layout), swap_inner(inner, layout)


def together(*values):
    return lax.optimization_barrier(values)


def edges(value):
    odd = lax.rem(lax.axis_index("space"), 2)
    cross = lax.dynamic_slice_in_dim(value, odd * ROW, ROW, 0)
    inner = lax.dynamic_slice_in_dim(value, (1 - odd) * ROW, ROW, 0)
    return cross, inner


def forward_project(a, w_qkv, layout):
    cross, inner = exchange(*edges(a), layout)
    block, width = a.shape
    (proj,) = call(
        project_kernel, "project", [(block, w_qkv.shape[1])], [VMEM] * 2, 2 * block * width * w_qkv.shape[1]
    )(a, w_qkv)
    return proj, cross, inner


def forward_pool(flags, proj, cross, inner, w_qkv, kern, layout):
    block = proj.shape[0]
    hidden = proj.shape[1] // 3
    kv, pk = call(
        pool_kernel, "pool", [(block, 2 * hidden), (block, hidden)], [SMEM] + [VMEM] * 5,
        2 * block * w_qkv.shape[0] * 2 * hidden, [pltpu.VMEM((256, 128), F32)],
    )(flags, cross, inner, w_qkv, proj, kern)
    return kv, pk


def attend(flags, tau, proj, kv, cross, inner, gb, w_out):
    block, width = gb.shape
    hidden = w_out.shape[0]
    return call(
        attention_kernel, "attention",
        [(block, hidden), (block, hidden), (block, 2 * hidden), (block, 2 * hidden)],
        [SMEM] * 2 + [VMEM] * 6, 2 * block * width * hidden * 3,
    )(flags, tau, proj, kv, cross, inner, gb, w_out)


def rebuild(att, w_out, b):
    block, width = b.shape
    return call(
        output_kernel, "output", [(block, width)], [VMEM] * 3, 2 * block * width * w_out.shape[0]
    )(att, w_out, b)[0]


def key_sums(flags, own, cross, inner, pk):
    block, channels = own.shape
    return call(
        key_kernel, "keys", [(block, channels), (ROW, channels), (ROW, channels)],
        [SMEM] + [VMEM] * 4, block * channels * 40,
    )(flags, own, cross, inner, pk)


def finish(flags, cross, gpool, inner, gq, w_qkv, kern, a, ga):
    block, width = a.shape
    columns = w_qkv.shape[1]
    return call(
        final_kernel, "final", [(block, width)], [SMEM] + [VMEM] * 8, 2 * block * width * columns,
        [
            pltpu.VMEM((256, 128), F32),
            pltpu.VMEM((block, columns), BF16),
            pltpu.VMEM((block, width), F32),
        ],
    )(flags, cross, gpool, inner, gq, w_qkv, kern, a, ga)[0]


def tile_flags(block_owner, layout):
    section = lax.axis_index("section")
    space = lax.axis_index("space")
    turned = jnp.zeros((), jnp.int32)
    for s in range(SECTIONS):
        for x in range(4):
            if layout(s, x):
                turned = turned | ((section == s) & (space // 4 == x)).astype(jnp.int32)
    tile = space ^ (2 * turned)
    odd = lax.rem(tile, 2)
    ids = jnp.arange(TILES, dtype=jnp.int32)
    lists_prev = jnp.any(block_owner == (ids - 1)[:, None], axis=1).astype(jnp.int32)
    lists_next = jnp.any(block_owner == (ids + 1)[:, None], axis=1).astype(jnp.int32)
    take = lambda v, i: jnp.sum(jnp.where(ids == i, v, 0))
    near_prev = take(lists_prev, tile)
    use_prev = take(lists_next, tile - 1)
    use_next = take(lists_prev, tile + 1)
    near_cross = jnp.where(odd == 1, 1 - near_prev, near_prev)
    use_cross = jnp.where(odd == 1, use_next, use_prev)
    use_inner = jnp.where(odd == 1, use_prev, use_next)
    return jnp.stack([near_cross, use_cross, use_inner, odd])


def body(top_a, top_b, grad_a, grad_b, w_qkv, w_out, kernel, tau, block_owner):
    a, b, ga, gb = top_a[0], top_b[0], grad_a[0], grad_b[0]
    w_qkv, w_out, kern, tau = w_qkv[0], w_out[0], kernel[0], tau[0]
    block = a.shape[0]
    one, two, start = first_layout, second_layout, start_layout
    flags1 = tile_flags(block_owner, one)
    flags2 = tile_flags(block_owner, two)

    proj1, cross, inner = forward_project(a, w_qkv, one)
    b2 = move(a, one, two, -1)
    ga2 = move(gb, one, two, -1)
    kv1, pk1 = forward_pool(flags1, proj1, cross, inner, w_qkv, kern, one)
    cross, inner = exchange(kv1, kv1, one)
    cross, inner, b2, ga2 = together(cross, inner, b2, ga2)
    att1, gq1, own1, near1 = attend(flags1, tau, proj1, kv1, cross, inner, gb, w_out)
    cross, inner = exchange(near1, near1, one)
    rebuilt1 = rebuild(att1, w_out, b)
    a2 = move(rebuilt1, one, two, -1)
    gpool1, cross, inner = key_sums(flags1, own1, cross, inner, pk1)
    cross, inner = exchange(cross, inner, one)
    new_grad1 = finish(flags1, cross, gpool1, inner, gq1, w_qkv, kern, a, ga)
    gb2 = move(new_grad1, one, two, -1)

    proj2, cross, inner = forward_project(a2, w_qkv, two)
    kv2, pk2 = forward_pool(flags2, proj2, cross, inner, w_qkv, kern, two)
    cross, inner = exchange(kv2, kv2, two)
    rebuilt_b = move(a2, two, start, -1)
    att2, gq2, own2, near2 = attend(flags2, tau, proj2, kv2, cross, inner, gb2, w_out)
    cross, inner = exchange(near2, near2, two)
    passed_a = move(gb2, two, start, -1)
    rebuilt2 = rebuild(att2, w_out, b2)
    rebuilt_a = move(rebuilt2, two, start, -1)
    gpool2, cross, inner = key_sums(flags2, own2, cross, inner, pk2)
    cross, inner = exchange(cross, inner, two)
    new_grad2 = finish(flags2, cross, gpool2, inner, gq2, w_qkv, kern, a2, ga2)
    passed_b = move(new_grad2, two, start, -1)
    return rebuilt_a[None], rebuilt_b[None], passed_a[None], passed_b[None]


def solution(mesh):
    state = P("section", "space", None)
    weights = P("section", None, None)
    return jax.shard_map(
        body,
        mesh=mesh,
        in_specs=(state,) * 4 + (weights,) * 3 + (P("section", None), P()),
        out_specs=(state,) * 4,
        check_vma=False,
    )
```

```python
import functools

import jax
import jax.numpy as jnp
from jax import lax
from jax.experimental import pallas as pl
from jax.experimental.pallas import tpu as pltpu
from jax.sharding import PartitionSpec as P

HEADS = 12
HEAD = 64
FT = 4
FW = 16
PAIRS = HEADS // 2
PW = 2 * HEAD
ROW = FT * FW

EPS_NORM = 1e-05
EPS_HEAD = 1e-06

F32 = jnp.float32
BF16 = jnp.bfloat16
VMEM = pltpu.VMEM
SMEM = pltpu.SMEM
HBM = pltpu.HBM
DMA = pltpu.SemaphoreType.DMA


def dot(a, b):
    return jnp.dot(a, b, preferred_element_type=F32)


def dot_nt(a, b):
    return lax.dot_general(a, b, (((1,), (1,)), ((), ())), preferred_element_type=F32)


def normalize_rows(features):
    average = jnp.mean(features, axis=-1, keepdims=True)
    centred = features - average
    inverse = lax.rsqrt(jnp.mean(centred * centred, axis=-1, keepdims=True) + EPS_NORM)
    return centred * inverse, inverse


def first_half(shape):
    return lax.broadcasted_iota(jnp.int32, shape, 1) < HEAD


def pair_sums(values, first):
    low = jnp.sum(jnp.where(first, values, 0.0), axis=-1, keepdims=True)
    high = jnp.sum(jnp.where(first, 0.0, values), axis=-1, keepdims=True)
    return jnp.where(first, low, high)


def pair_unit(values, first):
    inverse = lax.rsqrt(pair_sums(values * values, first) + EPS_HEAD)
    return values * inverse, inverse


def pair_unit_back(unit, inverse, gradient, first):
    return inverse * (gradient - unit * pair_sums(unit * gradient, first))


def pool_lanes(ext_ref, taps, flip, rows):
    column = lax.broadcasted_iota(jnp.int32, (FW, 128), 0)
    blocks = []
    for row in range(2):
        for frame in range(FT):
            parts = [None, None, None]
            for dr in range(3):
                if row + dr not in rows:
                    continue
                for df in range(3):
                    source = frame + df - 1
                    if source < 0 or source >= FT:
                        continue
                    start = (row + dr) * ROW + source * FW
                    block = ext_ref[start : start + FW, :]
                    for dc in range(3):
                        tap = dr * 9 + df * 3 + dc
                        term = taps[26 - tap if flip else tap] * block
                        parts[dc] = term if parts[dc] is None else parts[dc] + term
            left = jnp.where(column == 0, 0.0, pltpu.roll(parts[0], 1, 0))
            right = jnp.where(column == FW - 1, 0.0, pltpu.roll(parts[2], FW - 1, 0))
            blocks.append(parts[1] + left + right)
    return jnp.concatenate(blocks, axis=0)


def load_taps(kern_ref, lanes):
    return [jnp.broadcast_to(kern_ref[t, :, lanes], (FW, 128)) for t in range(27)]


def is_odd():
    return (lax.axis_index("space") & 1) == 1


def lists(owner_ref, row, tile):
    return (owner_ref[row, 0] == tile) | (owner_ref[row, 1] == tile)


def this_tile(layout):
    space = lax.axis_index("space")
    return space ^ (2 * layout(lax.axis_index("section"), space >> 2))


def stream(ref, buf, sems, cuts):
    copies = [pltpu.make_async_copy(ref.at[cut], buf.at[cut], sems.at[k]) for k, cut in enumerate(cuts)]
    for copy in copies:
        copy.start()

    def get(k):
        copies[k].wait()
        return buf[cuts[k]]

    return get


WHOLE = [(slice(None), slice(None))]


def project_kernel(a_ref, w_ref, out_ref):
    low = normalize_rows(a_ref[...].astype(F32))[0].astype(BF16)
    for c in range(0, w_ref.shape[1], 256):
        cut = slice(c, c + 256)
        out_ref[:, cut] = dot(low, w_ref[:, cut]).astype(BF16)


def first_project_kernel(a_ref, w_ref, out_ref, a_buf, w_buf, acc_ref, sems, w_sems):
    get_a = stream(a_ref, a_buf, sems, WHOLE)
    cuts = [(slice(r, r + 256), slice(None)) for r in range(0, w_ref.shape[0], 256)]
    get = stream(w_ref, w_buf, w_sems, cuts)
    low = normalize_rows(get_a(0).astype(F32))[0].astype(BF16)
    for k, (rows, _) in enumerate(cuts):
        piece = get(k)
        for c in range(0, w_ref.shape[1], 256):
            cut = slice(c, c + 256)
            total = dot(low[:, rows], piece[:, cut])
            if k:
                total = total + acc_ref[:, cut]
            if k + 1 < len(cuts):
                acc_ref[:, cut] = total
            else:
                out_ref[:, cut] = total.astype(BF16)


def pool_kernel(cross_ref, inner_ref, w_ref, proj_ref, kern_ref, kv_ref, pk_ref, ext_ref):
    hidden = pk_ref.shape[1]
    odd = is_odd()
    cross, inner = cross_ref[...], inner_ref[...]
    halo = jnp.concatenate(
        [jnp.where(odd, inner, cross), jnp.where(odd, cross, inner)], axis=0
    ).astype(F32)
    low = normalize_rows(halo)[0].astype(BF16)
    first = first_half((128, 128))
    for c in range(0, 2 * hidden, 256):
        outer = dot(low, w_ref[:, hidden + c : hidden + c + 256]).astype(BF16).astype(F32)
        for j in (0, 128):
            at = c + j
            ext_ref[0:ROW, :] = outer[:ROW, j : j + 128]
            ext_ref[ROW : ROW + 128, :] = proj_ref[:, hidden + at : hidden + at + 128].astype(F32)
            ext_ref[ROW + 128 :, :] = outer[ROW:, j : j + 128]
            pooled = pool_lanes(ext_ref, load_taps(kern_ref, slice(at, at + 128)), False, (0, 1, 2, 3)).astype(BF16)
            if at < hidden:
                pk_ref[:, at : at + 128] = pooled
                kv_ref[:, at : at + 128] = pair_unit(pooled.astype(F32), first)[0].astype(BF16)
            else:
                kv_ref[:, at : at + 128] = pooled


def attention_kernel(
    layout, owner_ref, tau_ref, proj_ref, own_ref, cross_ref, inner_ref, grad_ref,
    att_ref, gq_ref, part_own_ref, part_near_ref,
):
    hidden = att_ref.shape[1]
    tile = this_tile(layout)
    from_cross = lists(owner_ref, tile, tile - 1) ^ is_odd()
    first = first_half((128, 128))
    first_low = first_half((256, 128))

    def both(at):
        near = jnp.where(from_cross, cross_ref[:, at : at + PW], inner_ref[:, at : at + PW])
        return jnp.concatenate([own_ref[:, at : at + PW], near], axis=0)

    def masked(rows):
        zero = jnp.zeros_like(rows)
        return jnp.concatenate(
            [jnp.where(first_low, rows, zero), jnp.where(first_low, zero, rows)], axis=0
        )

    for p in range(PAIRS):
        at = p * PW
        g2 = grad_ref[:, at : at + PW]
        q_unit, q_inverse = pair_unit(proj_ref[:, at : at + PW].astype(F32), first)
        q_low = q_unit.astype(BF16)
        keys = masked(both(at))
        values = masked(both(hidden + at))
        scores = dot_nt(q_low, keys)
        grad_probs = dot_nt(g2, values)
        probs, grads = [], []
        for half in range(2):
            scale = tau_ref[2 * p + half]
            cut = slice(half * 256, half * 256 + 256)
            exponent = jnp.exp(scores[:, cut] * scale)
            prob = exponent * (1.0 / jnp.sum(exponent, axis=-1, keepdims=True))
            gp = grad_probs[:, cut]
            delta = jnp.sum(prob * gp, axis=-1, keepdims=True)
            probs.append(prob.astype(BF16))
            grads.append((scale * prob * (gp - delta)).astype(BF16))
        prob_low = jnp.concatenate(probs, axis=1)
        grad_scores = jnp.concatenate(grads, axis=1)
        att_ref[:, at : at + PW] = dot(prob_low, values).astype(BF16)
        grad_q = dot(grad_scores, keys)
        gq_ref[:, at : at + PW] = pair_unit_back(q_unit, q_inverse, grad_q, first).astype(BF16)
        grad_k = dot(grad_scores.T, q_low)
        grad_v = dot(prob_low.T, g2)
        grad_k = jnp.where(first_low, grad_k[:256], grad_k[256:]).astype(BF16)
        grad_v = jnp.where(first_low, grad_v[:256], grad_v[256:]).astype(BF16)
        part_own_ref[:, at : at + PW] = grad_k[:128]
        part_near_ref[:, at : at + PW] = grad_k[128:]
        part_own_ref[:, hidden + at : hidden + at + PW] = grad_v[:128]
        part_near_ref[:, hidden + at : hidden + at + PW] = grad_v[128:]


def attention_output_kernel(layout, *refs):
    ins, (wout_ref, b_ref), outs = refs[:7], refs[7:9], refs[9:13]
    out_ref, wout_buf, b_buf, sems = refs[13:]
    get_w = stream(wout_ref, wout_buf, sems.at[0], WHOLE)
    get_b = stream(b_ref, b_buf, sems.at[1], WHOLE)
    attention_kernel(layout, *ins, *outs)
    get_w(0)
    get_b(0)
    output_kernel(outs[0], wout_buf, b_buf, out_ref)


def settle_kernel(*refs):
    half = len(refs) // 2
    for source, target in zip(refs[:half], refs[half:]):
        target[...] = source[...]


def output_kernel(att_ref, wout_ref, b_ref, out_ref):
    att = att_ref[...]
    for c in range(0, out_ref.shape[1], 256):
        cut = slice(c, c + 256)
        out_ref[:, cut] = (b_ref[:, cut].astype(F32) - dot(att, wout_ref[:, cut])).astype(BF16)


def key_kernel(layout, owner_ref, own_ref, cross_ref, inner_ref, pk_ref, out_ref, cross_out_ref, inner_out_ref):
    hidden = pk_ref.shape[1]
    first = first_half((128, 128))
    odd = is_odd()
    tile = this_tile(layout)
    last = TILES - 1
    use_prev = (tile > 0) & lists(owner_ref, jnp.maximum(tile - 1, 0), tile)
    use_next = (tile < last) & lists(owner_ref, jnp.minimum(tile + 1, last), tile)
    use_cross = (odd & use_next) | (~odd & use_prev)
    use_inner = (odd & use_prev) | (~odd & use_next)
    for at in range(0, 2 * hidden, 128):
        cut = slice(at, at + 128)
        total = own_ref[:, cut].astype(F32)
        total = total + jnp.where(use_cross, cross_ref[:, cut].astype(F32), 0.0)
        total = total + jnp.where(use_inner, inner_ref[:, cut].astype(F32), 0.0)
        if at < hidden:
            unit, inverse = pair_unit(pk_ref[:, cut].astype(F32), first)
            total = pair_unit_back(unit, inverse, total, first)
        total = total.astype(BF16)
        out_ref[:, cut] = total
        cross_out_ref[:, cut] = jnp.where(odd, total[ROW:], total[:ROW])
        inner_out_ref[:, cut] = jnp.where(odd, total[:ROW], total[ROW:])


def local_kernel(own_ref, gq_ref, w_ref, kern_ref, part_ref, acc_ref, ext_ref):
    hidden = gq_ref.shape[1]
    gq = gq_ref[...]
    for at in range(0, 2 * hidden, 128):
        cut = slice(at, at + 128)
        ext_ref[ROW : ROW + 128, :] = own_ref[:, cut].astype(F32)
        part_ref[:, cut] = pool_lanes(ext_ref, load_taps(kern_ref, cut), True, (1, 2))
        acc_ref[:, cut] = dot_nt(gq, w_ref[cut, :hidden])


def final_kernel(
    cross_ref, inner_ref, part_ref, acc_ref, w_ref, kern_ref, a_ref, ga_ref,
    out_ref, ext_ref, gp_ref, sum_ref,
):
    odd = is_odd()
    channels = part_ref.shape[1]
    hidden = channels // 2
    width = a_ref.shape[1]
    for at in range(0, channels, 128):
        cut = slice(at, at + 128)
        cross, inner = cross_ref[:, cut], inner_ref[:, cut]
        ext_ref[0:ROW, :] = jnp.where(odd, inner, cross).astype(F32)
        ext_ref[ROW + 128 :, :] = jnp.where(odd, cross, inner).astype(F32)
        pooled = pool_lanes(ext_ref, load_taps(kern_ref, cut), True, (0, 3))
        gp_ref[:, cut] = (part_ref[:, cut] + pooled).astype(BF16)
    grad_raw = gp_ref[...]
    for c in range(0, width, 256):
        cut = slice(c, c + 256)
        sum_ref[:, cut] = acc_ref[:, cut] + dot_nt(grad_raw, w_ref[cut, hidden:])
    normalized, inverse = normalize_rows(a_ref[...].astype(F32))
    grad = sum_ref[...]
    grad_mean = jnp.mean(grad, axis=-1, keepdims=True)
    cross_mean = jnp.mean(grad * normalized, axis=-1, keepdims=True)
    back = inverse * (grad - grad_mean - normalized * cross_mean)
    out_ref[...] = (ga_ref[...].astype(F32) + back).astype(BF16)


def grad_kernel(gb_ref, wout_ref, out_ref):
    gb = gb_ref[...]
    for c in range(0, out_ref.shape[1], 256):
        out_ref[:, c : c + 256] = dot_nt(gb, wout_ref[c : c + 256, :]).astype(BF16)


def call(kernel, name, outs, specs, flops, scratch=(), kind=BF16, limit=6):
    def run(*args):
        moved = sum(x.size * x.dtype.itemsize for x in args)
        args = [
            pltpu.with_memory_space_constraint(x, HBM) if space == HBM else x
            for x, space in zip(args, specs)
        ]
        return pl.pallas_call(
            kernel,
            name=name,
            out_shape=[jax.ShapeDtypeStruct(s, kind) for s in outs],
            in_specs=[pl.BlockSpec(memory_space=s) for s in specs],
            out_specs=[pl.BlockSpec(memory_space=VMEM) for _ in outs],
            scratch_shapes=list(scratch),
            compiler_params=pltpu.CompilerParams(vmem_limit_bytes=limit * 1024 * 1024),
            cost_estimate=pl.CostEstimate(flops=flops, bytes_accessed=moved, transcendentals=0),
        )(*args)

    return run


SECTIONS = 16
TILES = 16


def start_layout(section, x):
    return 0


def first_layout(section, x):
    return 0


def second_layout(section, x):
    return ((section & 7) + 1) >> 3


def place(layout, section, tile):
    return section * TILES + (tile ^ (2 * layout(section, tile // 4)))


AXES = ("section", "space")


def move(value, source, target, by):
    pairs = [
        (place(source, s, t), place(target, (s + by) % SECTIONS, t))
        for s in range(SECTIONS)
        for t in range(TILES)
    ]
    return lax.ppermute(value, AXES, pairs)


def swap_cross(value, source, target):
    pairs = []
    for s in range(SECTIONS):
        for t in range(1, TILES - 1, 2):
            pairs.append((place(source, s, t), place(target, s, t + 1)))
            pairs.append((place(source, s, t + 1), place(target, s, t)))
    return lax.ppermute(value, AXES, pairs)


def swap_inner(value, source, target):
    pairs = [(place(source, s, t), place(target, s, t ^ 1)) for s in range(SECTIONS) for t in range(TILES)]
    return lax.ppermute(value, AXES, pairs)


def exchange(cross, inner, source, target=None):
    target = target or source
    inner = swap_inner(inner, source, target)
    return swap_cross(cross, source, target), inner


def together(*values):
    return lax.optimization_barrier(values)


def edges(value):
    odd = lax.rem(lax.axis_index("space"), 2)
    cross = lax.dynamic_slice_in_dim(value, odd * ROW, ROW, 0)
    inner = lax.dynamic_slice_in_dim(value, (1 - odd) * ROW, ROW, 0)
    return cross, inner


def forward_project(a, w_qkv, halo):
    cross, inner = halo
    block, width = a.shape
    (proj,) = call(
        project_kernel, "project", [(block, w_qkv.shape[1])], [VMEM] * 2, 2 * block * width * w_qkv.shape[1]
    )(a, w_qkv)
    return proj, cross, inner


def first_project(a, w_qkv):
    block, width = a.shape
    columns = w_qkv.shape[1]
    return call(
        first_project_kernel, "firstproject", [(block, columns)], [HBM] * 2, 2 * block * width * columns,
        [VMEM(a.shape, BF16), VMEM(w_qkv.shape, BF16), VMEM((block, columns), F32), DMA((1,)), DMA((width // 256,))],
        limit=14,
    )(a, w_qkv)[0]


def forward_pool(proj, cross, inner, w_qkv, kern):
    block = proj.shape[0]
    hidden = proj.shape[1] // 3
    return call(
        pool_kernel, "pool", [(block, 2 * hidden), (block, hidden)], [VMEM] * 5,
        2 * block * w_qkv.shape[0] * 2 * hidden, [VMEM((256, 128), F32)],
    )(cross, inner, w_qkv, proj, kern)


def grad_attended(gb, w_out):
    block, width = gb.shape
    hidden = w_out.shape[0]
    return call(
        grad_kernel, "gradatt", [(block, hidden)], [VMEM] * 2, 2 * block * width * hidden
    )(gb, w_out)[0]


def attend(layout, owner, tau, proj, kv, cross, inner, grad):
    block, hidden = grad.shape
    return call(
        functools.partial(attention_kernel, layout), "attention",
        [(block, hidden), (block, hidden), (block, 2 * hidden), (block, 2 * hidden)],
        [SMEM] * 2 + [VMEM] * 5, 2 * block * 512 * hidden * 8,
    )(owner, tau, proj, kv, cross, inner, grad)


def attend_rebuild(layout, owner, tau, proj, kv, cross, inner, grad, w_out, b):
    block, hidden = grad.shape
    return call(
        functools.partial(attention_output_kernel, layout), "attendout",
        [(block, hidden), (block, hidden), (block, 2 * hidden), (block, 2 * hidden), b.shape],
        [SMEM] * 2 + [VMEM] * 5 + [HBM] * 2, 2 * block * 512 * hidden * 8,
        [VMEM(w_out.shape, BF16), VMEM(b.shape, BF16), DMA((2, 1))],
        limit=9,
    )(owner, tau, proj, kv, cross, inner, grad, w_out, b)


def settle(*values):
    return call(settle_kernel, "settle", [v.shape for v in values], [VMEM] * len(values), 1)(*values)


def rebuild(att, w_out, b):
    block, width = b.shape
    return call(
        output_kernel, "output", [(block, width)], [VMEM] * 3, 2 * block * width * w_out.shape[0]
    )(att, w_out, b)[0]


def key_sums(layout, owner, own, cross, inner, pk):
    block, channels = own.shape
    return call(
        functools.partial(key_kernel, layout), "keys",
        [(block, channels), (ROW, channels), (ROW, channels)],
        [SMEM] + [VMEM] * 4, block * channels * 40,
    )(owner, own, cross, inner, pk)


def finish_local(gpool, gq, w_qkv, kern):
    block, channels = gpool.shape
    width = w_qkv.shape[0]
    return call(
        local_kernel, "local", [(block, channels), (block, width)], [VMEM] * 4,
        2 * block * width * gq.shape[1], [VMEM((256, 128), F32)], F32,
    )(gpool, gq, w_qkv, kern)


def finish(cross, inner, part, acc, w_qkv, kern, a, ga):
    block, width = a.shape
    channels = part.shape[1]
    return call(
        final_kernel, "final", [(block, width)], [VMEM] * 8, 2 * block * width * channels,
        [
            VMEM((256, 128), F32),
            VMEM((block, channels), BF16),
            VMEM((block, width), F32),
        ],
    )(cross, inner, part, acc, w_qkv, kern, a, ga)[0]


def body(top_a, top_b, grad_a, grad_b, w_qkv, w_out, kernel, tau, owner):
    a, b, ga, gb = top_a[0], top_b[0], grad_a[0], grad_b[0]
    w_qkv, w_out, tau = w_qkv[0], w_out[0], tau[0]
    kern = jnp.transpose(kernel, (1, 0, 2))
    one, two, start = first_layout, second_layout, start_layout

    halo = exchange(*edges(a), start, one)
    b2 = move(a, one, two, -1)
    ga2 = move(gb, one, two, -1)
    proj1 = first_project(a, w_qkv)
    cross, inner = halo
    kv1, pk1 = forward_pool(proj1, cross, inner, w_qkv, kern)
    cross, inner = exchange(kv1, kv1, one)
    grad1 = grad_attended(gb, w_out)
    cross, inner, b2, ga2, grad1 = together(cross, inner, b2, ga2, grad1)
    _, gq1, own1, near1, rebuilt1 = attend_rebuild(
        one, owner, tau, proj1, kv1, cross, inner, grad1, w_out, b
    )
    cross, inner = exchange(near1, near1, one)
    a2 = move(rebuilt1, one, two, -1)
    gpool1, cross, inner = key_sums(one, owner, own1, cross, inner, pk1)
    cross, inner = exchange(cross, inner, one)
    part1, acc1 = finish_local(gpool1, gq1, w_qkv, kern)
    new_grad1 = finish(cross, inner, part1, acc1, w_qkv, kern, a, ga)

    proj2, cross, inner = forward_project(a2, w_qkv, exchange(*edges(a2), two))
    kv2, pk2 = forward_pool(proj2, cross, inner, w_qkv, kern)
    kv2, new_grad1 = together(kv2, new_grad1)
    gb2 = move(new_grad1, one, two, -1)
    cross, inner = exchange(kv2, kv2, two)
    grad2 = grad_attended(gb2, w_out)
    passed_a = move(gb2, two, start, -1)
    att2, gq2, own2, near2 = attend(two, owner, tau, proj2, kv2, cross, inner, grad2)
    cross, inner = exchange(near2, near2, two)
    att2, passed_a = together(att2, passed_a)
    rebuilt2 = rebuild(att2, w_out, b2)
    cross, inner, rebuilt2, late = together(cross, inner, rebuilt2, a2)
    rebuilt_b = move(late, two, start, -1)
    gpool2, cross, inner = key_sums(two, owner, own2, cross, inner, pk2)
    cross, inner = exchange(cross, inner, two)
    part2, acc2 = finish_local(gpool2, gq2, w_qkv, kern)
    cross, inner, rebuilt2, rebuilt_b = together(cross, inner, rebuilt2, rebuilt_b)
    rebuilt_a = move(rebuilt2, two, start, -1)
    new_grad2 = finish(cross, inner, part2, acc2, w_qkv, kern, a2, ga2)
    passed_b = move(new_grad2, two, start, -1)
    rebuilt_a, rebuilt_b, passed_a = settle(rebuilt_a, rebuilt_b, passed_a)
    return rebuilt_a[None], rebuilt_b[None], passed_a[None], passed_b[None]


def solution(mesh):
    state = P("section", "space", None)
    weights = P("section", None, None)
    return jax.shard_map(
        body,
        mesh=mesh,
        in_specs=(state,) * 4 + (weights,) * 3 + (P("section", None), P()),
        out_specs=(state,) * 4,
        check_vma=False,
    )
```

```python
import functools

import jax
import jax.numpy as jnp
from jax import lax
from jax.experimental import pallas as pl
from jax.experimental.pallas import tpu as pltpu
from jax.sharding import PartitionSpec as P

HEADS = 12
HEAD = 64
FT = 4
FW = 16
PAIRS = HEADS // 2
PW = 2 * HEAD
ROW = FT * FW

EPS_NORM = 1e-05
EPS_HEAD = 1e-06

F32 = jnp.float32
BF16 = jnp.bfloat16
VMEM = pltpu.VMEM
SMEM = pltpu.SMEM
HBM = pltpu.HBM
DMA = pltpu.SemaphoreType.DMA


def dot(a, b):
    return jnp.dot(a, b, preferred_element_type=F32)


def dot_nt(a, b):
    return lax.dot_general(a, b, (((1,), (1,)), ((), ())), preferred_element_type=F32)


def normalize_rows(features):
    average = jnp.mean(features, axis=-1, keepdims=True)
    centred = features - average
    inverse = lax.rsqrt(jnp.mean(centred * centred, axis=-1, keepdims=True) + EPS_NORM)
    return centred * inverse, inverse


def first_half(shape):
    return lax.broadcasted_iota(jnp.int32, shape, 1) < HEAD


def pair_sums(values, first):
    low = jnp.sum(jnp.where(first, values, 0.0), axis=-1, keepdims=True)
    high = jnp.sum(jnp.where(first, 0.0, values), axis=-1, keepdims=True)
    return jnp.where(first, low, high)


def pair_unit(values, first):
    inverse = lax.rsqrt(pair_sums(values * values, first) + EPS_HEAD)
    return values * inverse, inverse


def pair_unit_back(unit, inverse, gradient, first):
    return inverse * (gradient - unit * pair_sums(unit * gradient, first))


def pool_lanes(ext_ref, taps, flip, rows):
    column = lax.broadcasted_iota(jnp.int32, (FW, 128), 0)
    blocks = []
    for row in range(2):
        for frame in range(FT):
            parts = [None, None, None]
            for dr in range(3):
                if row + dr not in rows:
                    continue
                for df in range(3):
                    source = frame + df - 1
                    if source < 0 or source >= FT:
                        continue
                    start = (row + dr) * ROW + source * FW
                    block = ext_ref[start : start + FW, :]
                    for dc in range(3):
                        tap = dr * 9 + df * 3 + dc
                        term = taps[26 - tap if flip else tap] * block
                        parts[dc] = term if parts[dc] is None else parts[dc] + term
            left = jnp.where(column == 0, 0.0, pltpu.roll(parts[0], 1, 0))
            right = jnp.where(column == FW - 1, 0.0, pltpu.roll(parts[2], FW - 1, 0))
            blocks.append(parts[1] + left + right)
    return jnp.concatenate(blocks, axis=0)


def load_taps(kern_ref, lanes):
    return [jnp.broadcast_to(kern_ref[t, :, lanes], (FW, 128)) for t in range(27)]


def is_odd():
    return (lax.axis_index("space") & 1) == 1


def lists(owner_ref, row, tile):
    return (owner_ref[row, 0] == tile) | (owner_ref[row, 1] == tile)


def this_tile(layout):
    space = lax.axis_index("space")
    return space ^ (2 * layout(lax.axis_index("section"), space >> 2))


def stream(ref, buf, sems, cuts):
    copies = [pltpu.make_async_copy(ref.at[cut], buf.at[cut], sems.at[k]) for k, cut in enumerate(cuts)]
    for copy in copies:
        copy.start()

    def get(k):
        copies[k].wait()
        return buf[cuts[k]]

    return get


WHOLE = [(slice(None), slice(None))]


def put_projected(q_ref, raw_ref, c, value):
    hidden = q_ref.shape[1]
    if c < hidden:
        q_ref[:, c : c + 256] = value.astype(BF16)
    else:
        raw_ref[:, c - hidden : c - hidden + 256] = value.astype(BF16)


def project_kernel(a_ref, w_ref, q_ref, raw_ref):
    low = normalize_rows(a_ref[...].astype(F32))[0].astype(BF16)
    for c in range(0, w_ref.shape[1], 256):
        put_projected(q_ref, raw_ref, c, dot(low, w_ref[:, c : c + 256]))


def first_project_kernel(a_ref, w_ref, q_ref, raw_ref, a_buf, w_buf, acc_ref, sems, w_sems):
    get_a = stream(a_ref, a_buf, sems, WHOLE)
    cuts = [(slice(r, r + 256), slice(None)) for r in range(0, w_ref.shape[0], 256)]
    get = stream(w_ref, w_buf, w_sems, cuts)
    low = normalize_rows(get_a(0).astype(F32))[0].astype(BF16)
    for k, (rows, _) in enumerate(cuts):
        piece = get(k)
        for c in range(0, w_ref.shape[1], 256):
            cut = slice(c, c + 256)
            total = dot(low[:, rows], piece[:, cut])
            if k:
                total = total + acc_ref[:, cut]
            if k + 1 < len(cuts):
                acc_ref[:, cut] = total
            else:
                put_projected(q_ref, raw_ref, c, total)


def pool_kernel(cross_ref, inner_ref, w_ref, raw_ref, kern_ref, kv_ref, pk_ref, ext_ref):
    hidden = pk_ref.shape[1]
    odd = is_odd()
    cross, inner = cross_ref[...], inner_ref[...]
    halo = jnp.concatenate(
        [jnp.where(odd, inner, cross), jnp.where(odd, cross, inner)], axis=0
    ).astype(F32)
    low = normalize_rows(halo)[0].astype(BF16)
    first = first_half((128, 128))
    for c in range(0, 2 * hidden, 256):
        outer = dot(low, w_ref[:, hidden + c : hidden + c + 256]).astype(BF16).astype(F32)
        for j in (0, 128):
            at = c + j
            ext_ref[0:ROW, :] = outer[:ROW, j : j + 128]
            ext_ref[ROW : ROW + 128, :] = raw_ref[:, at : at + 128].astype(F32)
            ext_ref[ROW + 128 :, :] = outer[ROW:, j : j + 128]
            pooled = pool_lanes(ext_ref, load_taps(kern_ref, slice(at, at + 128)), False, (0, 1, 2, 3)).astype(BF16)
            if at < hidden:
                pk_ref[:, at : at + 128] = pooled
                kv_ref[:, at : at + 128] = pair_unit(pooled.astype(F32), first)[0].astype(BF16)
            else:
                kv_ref[:, at : at + 128] = pooled


def attention_kernel(
    layout, owner_ref, tau_ref, proj_ref, own_ref, cross_ref, inner_ref, grad_ref,
    att_ref, gq_ref, part_own_ref, part_near_ref,
):
    hidden = att_ref.shape[1]
    tile = this_tile(layout)
    from_cross = lists(owner_ref, tile, tile - 1) ^ is_odd()
    first = first_half((128, 128))
    first_low = first_half((256, 128))

    def both(at):
        near = jnp.where(from_cross, cross_ref[:, at : at + PW], inner_ref[:, at : at + PW])
        return jnp.concatenate([own_ref[:, at : at + PW], near], axis=0)

    def masked(rows):
        zero = jnp.zeros_like(rows)
        return jnp.concatenate(
            [jnp.where(first_low, rows, zero), jnp.where(first_low, zero, rows)], axis=0
        )

    for p in range(PAIRS):
        at = p * PW
        g2 = grad_ref[:, at : at + PW]
        q_unit, q_inverse = pair_unit(proj_ref[:, at : at + PW].astype(F32), first)
        q_low = q_unit.astype(BF16)
        keys = masked(both(at))
        values = masked(both(hidden + at))
        scores = dot_nt(keys, q_low)
        grad_probs = dot_nt(values, g2)
        probs, grads = [], []
        for half in range(2):
            scale = tau_ref[2 * p + half]
            cut = slice(half * 256, half * 256 + 256)
            exponent = jnp.exp(scores[cut] * scale)
            prob = exponent * (1.0 / jnp.sum(exponent, axis=0, keepdims=True))
            gp = grad_probs[cut]
            delta = jnp.sum(prob * gp, axis=0, keepdims=True)
            probs.append(prob.astype(BF16))
            grads.append((scale * prob * (gp - delta)).astype(BF16))
        prob_low = jnp.concatenate(probs, axis=0)
        grad_scores = jnp.concatenate(grads, axis=0)
        att_ref[:, at : at + PW] = dot(values.T, prob_low).T.astype(BF16)
        grad_q = dot(keys.T, grad_scores).T
        gq_ref[:, at : at + PW] = pair_unit_back(q_unit, q_inverse, grad_q, first).astype(BF16)
        grad_k = dot(grad_scores, q_low)
        grad_v = dot(prob_low, g2)
        grad_k = jnp.where(first_low, grad_k[:256], grad_k[256:]).astype(BF16)
        grad_v = jnp.where(first_low, grad_v[:256], grad_v[256:]).astype(BF16)
        part_own_ref[:, at : at + PW] = grad_k[:128]
        part_near_ref[:, at : at + PW] = grad_k[128:]
        part_own_ref[:, hidden + at : hidden + at + PW] = grad_v[:128]
        part_near_ref[:, hidden + at : hidden + at + PW] = grad_v[128:]


def attention_output_kernel(layout, *refs):
    ins, (wout_ref, b_ref), outs = refs[:7], refs[7:9], refs[9:13]
    out_ref, wout_buf, b_buf, sems = refs[13:]
    get_w = stream(wout_ref, wout_buf, sems.at[0], WHOLE)
    get_b = stream(b_ref, b_buf, sems.at[1], WHOLE)
    attention_kernel(layout, *ins, *outs)
    get_w(0)
    get_b(0)
    output_kernel(outs[0], wout_buf, b_buf, out_ref)


def settle_kernel(*refs):
    half = len(refs) // 2
    for source, target in zip(refs[:half], refs[half:]):
        target[...] = source[...]


def output_kernel(att_ref, wout_ref, b_ref, out_ref):
    att = att_ref[...]
    for c in range(0, out_ref.shape[1], 256):
        cut = slice(c, c + 256)
        out_ref[:, cut] = (b_ref[:, cut].astype(F32) - dot(att, wout_ref[:, cut])).astype(BF16)


def key_kernel(layout, owner_ref, own_ref, cross_ref, inner_ref, pk_ref, out_ref, cross_out_ref, inner_out_ref):
    hidden = pk_ref.shape[1]
    first = first_half((128, 128))
    odd = is_odd()
    tile = this_tile(layout)
    last = TILES - 1
    use_prev = (tile > 0) & lists(owner_ref, jnp.maximum(tile - 1, 0), tile)
    use_next = (tile < last) & lists(owner_ref, jnp.minimum(tile + 1, last), tile)
    use_cross = (odd & use_next) | (~odd & use_prev)
    use_inner = (odd & use_prev) | (~odd & use_next)
    for at in range(0, 2 * hidden, 128):
        cut = slice(at, at + 128)
        total = own_ref[:, cut].astype(F32)
        total = total + jnp.where(use_cross, cross_ref[:, cut].astype(F32), 0.0)
        total = total + jnp.where(use_inner, inner_ref[:, cut].astype(F32), 0.0)
        if at < hidden:
            unit, inverse = pair_unit(pk_ref[:, cut].astype(F32), first)
            total = pair_unit_back(unit, inverse, total, first)
        total = total.astype(BF16)
        out_ref[:, cut] = total
        cross_out_ref[:, cut] = jnp.where(odd, total[ROW:], total[:ROW])
        inner_out_ref[:, cut] = jnp.where(odd, total[:ROW], total[ROW:])


def local_kernel(own_ref, gq_ref, w_ref, kern_ref, part_ref, acc_ref, ext_ref):
    hidden = gq_ref.shape[1]
    gq = gq_ref[...]
    for at in range(0, 2 * hidden, 128):
        cut = slice(at, at + 128)
        ext_ref[ROW : ROW + 128, :] = own_ref[:, cut].astype(F32)
        part_ref[:, cut] = pool_lanes(ext_ref, load_taps(kern_ref, cut), True, (1, 2))
        acc_ref[:, cut] = dot_nt(gq, w_ref[cut, :hidden])


def final_kernel(
    cross_ref, inner_ref, part_ref, acc_ref, w_ref, kern_ref, a_ref, ga_ref,
    out_ref, ext_ref, gp_ref, sum_ref,
):
    odd = is_odd()
    channels = part_ref.shape[1]
    hidden = channels // 2
    width = a_ref.shape[1]
    for at in range(0, channels, 128):
        cut = slice(at, at + 128)
        cross, inner = cross_ref[:, cut], inner_ref[:, cut]
        ext_ref[0:ROW, :] = jnp.where(odd, inner, cross).astype(F32)
        ext_ref[ROW + 128 :, :] = jnp.where(odd, cross, inner).astype(F32)
        pooled = pool_lanes(ext_ref, load_taps(kern_ref, cut), True, (0, 3))
        gp_ref[:, cut] = (part_ref[:, cut] + pooled).astype(BF16)
    grad_raw = gp_ref[...]
    for c in range(0, width, 256):
        cut = slice(c, c + 256)
        sum_ref[:, cut] = acc_ref[:, cut] + dot_nt(grad_raw, w_ref[cut, hidden:])
    normalized, inverse = normalize_rows(a_ref[...].astype(F32))
    grad = sum_ref[...]
    grad_mean = jnp.mean(grad, axis=-1, keepdims=True)
    cross_mean = jnp.mean(grad * normalized, axis=-1, keepdims=True)
    back = inverse * (grad - grad_mean - normalized * cross_mean)
    out_ref[...] = (ga_ref[...].astype(F32) + back).astype(BF16)


def grad_kernel(gb_ref, wout_ref, out_ref):
    gb = gb_ref[...]
    for c in range(0, out_ref.shape[1], 256):
        out_ref[:, c : c + 256] = dot_nt(gb, wout_ref[c : c + 256, :]).astype(BF16)


def call(kernel, name, outs, specs, flops, scratch=(), kind=BF16, limit=6):
    def run(*args):
        moved = sum(x.size * x.dtype.itemsize for x in args)
        args = [
            pltpu.with_memory_space_constraint(x, HBM) if space == HBM else x
            for x, space in zip(args, specs)
        ]
        return pl.pallas_call(
            kernel,
            name=name,
            out_shape=[jax.ShapeDtypeStruct(s, kind) for s in outs],
            in_specs=[pl.BlockSpec(memory_space=s) for s in specs],
            out_specs=[pl.BlockSpec(memory_space=VMEM) for _ in outs],
            scratch_shapes=list(scratch),
            compiler_params=pltpu.CompilerParams(vmem_limit_bytes=limit * 1024 * 1024),
            cost_estimate=pl.CostEstimate(flops=flops, bytes_accessed=moved, transcendentals=0),
        )(*args)

    return run


SECTIONS = 16
TILES = 16


def start_layout(section, x):
    return 0


def first_layout(section, x):
    return 0


def second_layout(section, x):
    return ((section & 7) + 1) >> 3


def place(layout, section, tile):
    return section * TILES + (tile ^ (2 * layout(section, tile // 4)))


AXES = ("section", "space")


def move(value, source, target, by):
    pairs = [
        (place(source, s, t), place(target, (s + by) % SECTIONS, t))
        for s in range(SECTIONS)
        for t in range(TILES)
    ]
    return lax.ppermute(value, AXES, pairs)


def swap_cross(value, source, target):
    pairs = []
    for s in range(SECTIONS):
        for t in range(1, TILES - 1, 2):
            pairs.append((place(source, s, t), place(target, s, t + 1)))
            pairs.append((place(source, s, t + 1), place(target, s, t)))
    return lax.ppermute(value, AXES, pairs)


def swap_inner(value, source, target):
    pairs = [(place(source, s, t), place(target, s, t ^ 1)) for s in range(SECTIONS) for t in range(TILES)]
    return lax.ppermute(value, AXES, pairs)


def exchange(cross, inner, source, target=None):
    target = target or source
    inner = swap_inner(inner, source, target)
    return swap_cross(cross, source, target), inner


def together(*values):
    return lax.optimization_barrier(values)


def edges(value):
    odd = lax.rem(lax.axis_index("space"), 2)
    cross = lax.dynamic_slice_in_dim(value, odd * ROW, ROW, 0)
    inner = lax.dynamic_slice_in_dim(value, (1 - odd) * ROW, ROW, 0)
    return cross, inner


def forward_project(a, w_qkv):
    block, width = a.shape
    columns = w_qkv.shape[1]
    return call(
        project_kernel, "project", [(block, columns // 3), (block, columns // 3 * 2)], [VMEM] * 2,
        2 * block * width * columns,
    )(a, w_qkv)


def first_project(a, w_qkv):
    block, width = a.shape
    columns = w_qkv.shape[1]
    return call(
        first_project_kernel, "firstproject", [(block, columns // 3), (block, columns // 3 * 2)], [HBM] * 2, 2 * block * width * columns,
        [VMEM(a.shape, BF16), VMEM(w_qkv.shape, BF16), VMEM((block, columns), F32), DMA((1,)), DMA((width // 256,))],
        limit=14,
    )(a, w_qkv)


def forward_pool(raw, cross, inner, w_qkv, kern):
    block, channels = raw.shape
    hidden = channels // 2
    return call(
        pool_kernel, "pool", [(block, 2 * hidden), (block, hidden)], [VMEM] * 5,
        2 * block * w_qkv.shape[0] * 2 * hidden, [VMEM((256, 128), F32)],
    )(cross, inner, w_qkv, raw, kern)


def grad_attended(gb, w_out):
    block, width = gb.shape
    hidden = w_out.shape[0]
    return call(
        grad_kernel, "gradatt", [(block, hidden)], [VMEM] * 2, 2 * block * width * hidden
    )(gb, w_out)[0]


def attend(layout, owner, tau, proj, kv, cross, inner, grad):
    block, hidden = grad.shape
    return call(
        functools.partial(attention_kernel, layout), "attention",
        [(block, hidden), (block, hidden), (block, 2 * hidden), (block, 2 * hidden)],
        [SMEM] * 2 + [VMEM] * 5, 2 * block * 512 * hidden * 8,
    )(owner, tau, proj, kv, cross, inner, grad)


def attend_rebuild(layout, owner, tau, proj, kv, cross, inner, grad, w_out, b):
    block, hidden = grad.shape
    return call(
        functools.partial(attention_output_kernel, layout), "attendout",
        [(block, hidden), (block, hidden), (block, 2 * hidden), (block, 2 * hidden), b.shape],
        [SMEM] * 2 + [VMEM] * 5 + [HBM] * 2, 2 * block * 512 * hidden * 8,
        [VMEM(w_out.shape, BF16), VMEM(b.shape, BF16), DMA((2, 1))],
        limit=9,
    )(owner, tau, proj, kv, cross, inner, grad, w_out, b)


def settle(*values):
    return call(settle_kernel, "settle", [v.shape for v in values], [VMEM] * len(values), 1)(*values)


def rebuild(att, w_out, b):
    block, width = b.shape
    return call(
        output_kernel, "output", [(block, width)], [VMEM] * 3, 2 * block * width * w_out.shape[0]
    )(att, w_out, b)[0]


def key_sums(layout, owner, own, cross, inner, pk):
    block, channels = own.shape
    return call(
        functools.partial(key_kernel, layout), "keys",
        [(block, channels), (ROW, channels), (ROW, channels)],
        [SMEM] + [VMEM] * 4, block * channels * 40,
    )(owner, own, cross, inner, pk)


def finish_local(gpool, gq, w_qkv, kern):
    block, channels = gpool.shape
    width = w_qkv.shape[0]
    return call(
        local_kernel, "local", [(block, channels), (block, width)], [VMEM] * 4,
        2 * block * width * gq.shape[1], [VMEM((256, 128), F32)], F32,
    )(gpool, gq, w_qkv, kern)


def finish(cross, inner, part, acc, w_qkv, kern, a, ga):
    block, width = a.shape
    channels = part.shape[1]
    return call(
        final_kernel, "final", [(block, width)], [VMEM] * 8, 2 * block * width * channels,
        [
            VMEM((256, 128), F32),
            VMEM((block, channels), BF16),
            VMEM((block, width), F32),
        ],
    )(cross, inner, part, acc, w_qkv, kern, a, ga)[0]


def body(top_a, top_b, grad_a, grad_b, w_qkv, w_out, kernel, tau, owner):
    a, b, ga, gb = top_a[0], top_b[0], grad_a[0], grad_b[0]
    w_qkv, w_out, tau = w_qkv[0], w_out[0], tau[0]
    kern = jnp.transpose(kernel, (1, 0, 2))
    one, two, start = first_layout, second_layout, start_layout

    halo = exchange(*edges(a), start, one)
    q1, raw1 = first_project(a, w_qkv)
    cross, inner = halo
    kv1, pk1 = forward_pool(raw1, cross, inner, w_qkv, kern)
    kv1, a_pass, gb_pass = together(kv1, a, gb)
    cross, inner = exchange(kv1, kv1, one)
    b2 = move(a_pass, one, two, -1)
    ga2 = move(gb_pass, one, two, -1)
    grad1 = grad_attended(gb, w_out)
    cross, inner, grad1 = together(cross, inner, grad1)
    _, gq1, own1, near1, rebuilt1 = attend_rebuild(
        one, owner, tau, q1, kv1, cross, inner, grad1, w_out, b
    )
    near1, b2, ga2 = together(near1, b2, ga2)
    cross, inner = exchange(near1, near1, one)
    a2 = move(rebuilt1, one, two, -1)
    gpool1, cross, inner = key_sums(one, owner, own1, cross, inner, pk1)
    cross, inner = exchange(cross, inner, one)
    part1, acc1 = finish_local(gpool1, gq1, w_qkv, kern)
    new_grad1 = finish(cross, inner, part1, acc1, w_qkv, kern, a, ga)

    cross, inner = exchange(*edges(a2), two)
    q2, raw2 = forward_project(a2, w_qkv)
    kv2, pk2 = forward_pool(raw2, cross, inner, w_qkv, kern)
    kv2, new_grad1 = together(kv2, new_grad1)
    gb2 = move(new_grad1, one, two, -1)
    cross, inner = exchange(kv2, kv2, two)
    grad2 = grad_attended(gb2, w_out)
    passed_a = move(gb2, two, start, -1)
    att2, gq2, own2, near2 = attend(two, owner, tau, q2, kv2, cross, inner, grad2)
    cross, inner = exchange(near2, near2, two)
    att2, passed_a = together(att2, passed_a)
    rebuilt2 = rebuild(att2, w_out, b2)
    cross, inner, rebuilt2, late = together(cross, inner, rebuilt2, a2)
    rebuilt_b = move(late, two, start, -1)
    gpool2, cross, inner = key_sums(two, owner, own2, cross, inner, pk2)
    cross, inner = exchange(cross, inner, two)
    part2, acc2 = finish_local(gpool2, gq2, w_qkv, kern)
    cross, inner, rebuilt2, rebuilt_b = together(cross, inner, rebuilt2, rebuilt_b)
    rebuilt_a = move(rebuilt2, two, start, -1)
    new_grad2 = finish(cross, inner, part2, acc2, w_qkv, kern, a2, ga2)
    passed_b = move(new_grad2, two, start, -1)
    rebuilt_a, rebuilt_b, passed_a = settle(rebuilt_a, rebuilt_b, passed_a)
    return rebuilt_a[None], rebuilt_b[None], passed_a[None], passed_b[None]


def solution(mesh):
    state = P("section", "space", None)
    weights = P("section", None, None)
    return jax.shard_map(
        body,
        mesh=mesh,
        in_specs=(state,) * 4 + (weights,) * 3 + (P("section", None), P()),
        out_specs=(state,) * 4,
        check_vma=False,
    )
```

```python
import functools

import jax
import jax.numpy as jnp
from jax import lax
from jax.experimental import pallas as pl
from jax.experimental.pallas import tpu as pltpu
from jax.sharding import PartitionSpec as P

HEADS = 12
HEAD = 64
FT = 4
FW = 16
PAIRS = HEADS // 2
PW = 2 * HEAD
ROW = FT * FW

EPS_NORM = 1e-05
EPS_HEAD = 1e-06

F32 = jnp.float32
BF16 = jnp.bfloat16
VMEM = pltpu.VMEM
SMEM = pltpu.SMEM
HBM = pltpu.HBM
DMA = pltpu.SemaphoreType.DMA


def dot(a, b):
    return jnp.dot(a, b, preferred_element_type=F32)


def dot_nt(a, b):
    return lax.dot_general(a, b, (((1,), (1,)), ((), ())), preferred_element_type=F32)


def normalize_rows(features):
    average = jnp.mean(features, axis=-1, keepdims=True)
    centred = features - average
    inverse = lax.rsqrt(jnp.mean(centred * centred, axis=-1, keepdims=True) + EPS_NORM)
    return centred * inverse, inverse


def first_half(shape):
    return lax.broadcasted_iota(jnp.int32, shape, 1) < HEAD


def pair_sums(values, first):
    low = jnp.sum(jnp.where(first, values, 0.0), axis=-1, keepdims=True)
    high = jnp.sum(jnp.where(first, 0.0, values), axis=-1, keepdims=True)
    return jnp.where(first, low, high)


def pair_unit(values, first):
    inverse = lax.rsqrt(pair_sums(values * values, first) + EPS_HEAD)
    return values * inverse, inverse


def pair_unit_back(unit, inverse, gradient, first):
    return inverse * (gradient - unit * pair_sums(unit * gradient, first))


def pool_lanes(ext_ref, taps, flip, rows):
    column = lax.broadcasted_iota(jnp.int32, (FW, 128), 0)
    blocks = []
    for row in range(2):
        for frame in range(FT):
            parts = [None, None, None]
            for dr in range(3):
                if row + dr not in rows:
                    continue
                for df in range(3):
                    source = frame + df - 1
                    if source < 0 or source >= FT:
                        continue
                    start = (row + dr) * ROW + source * FW
                    block = ext_ref[start : start + FW, :]
                    for dc in range(3):
                        tap = dr * 9 + df * 3 + dc
                        term = taps[26 - tap if flip else tap] * block
                        parts[dc] = term if parts[dc] is None else parts[dc] + term
            left = jnp.where(column == 0, 0.0, pltpu.roll(parts[0], 1, 0))
            right = jnp.where(column == FW - 1, 0.0, pltpu.roll(parts[2], FW - 1, 0))
            blocks.append(parts[1] + left + right)
    return jnp.concatenate(blocks, axis=0)


def load_taps(kern_ref, lanes):
    return [jnp.broadcast_to(kern_ref[t, :, lanes], (FW, 128)) for t in range(27)]


def is_odd():
    return (lax.axis_index("space") & 1) == 1


def lists(owner_ref, row, tile):
    return (owner_ref[row, 0] == tile) | (owner_ref[row, 1] == tile)


def this_tile(layout):
    space = lax.axis_index("space")
    return space ^ (2 * layout(lax.axis_index("section"), space >> 2))


def stream(ref, buf, sems, cuts):
    copies = [pltpu.make_async_copy(ref.at[cut], buf.at[cut], sems.at[k]) for k, cut in enumerate(cuts)]
    for copy in copies:
        copy.start()

    def get(k):
        copies[k].wait()
        return buf[cuts[k]]

    return get


WHOLE = [(slice(None), slice(None))]


def project_kernel(a_ref, w_ref, out_ref):
    low = normalize_rows(a_ref[...].astype(F32))[0].astype(BF16)
    for c in range(0, w_ref.shape[1], 256):
        cut = slice(c, c + 256)
        out_ref[:, cut] = dot(low, w_ref[:, cut]).astype(BF16)


def first_project_kernel(a_ref, w_ref, out_ref, a_buf, w_buf, acc_ref, sems, w_sems):
    get_a = stream(a_ref, a_buf, sems, WHOLE)
    cuts = [(slice(r, r + 256), slice(None)) for r in range(0, w_ref.shape[0], 256)]
    get = stream(w_ref, w_buf, w_sems, cuts)
    low = normalize_rows(get_a(0).astype(F32))[0].astype(BF16)
    for k, (rows, _) in enumerate(cuts):
        piece = get(k)
        for c in range(0, w_ref.shape[1], 256):
            cut = slice(c, c + 256)
            total = dot(low[:, rows], piece[:, cut])
            if k:
                total = total + acc_ref[:, cut]
            if k + 1 < len(cuts):
                acc_ref[:, cut] = total
            else:
                out_ref[:, cut] = total.astype(BF16)


def pool_kernel(cross_ref, inner_ref, w_ref, proj_ref, kern_ref, kv_ref, pk_ref, ext_ref):
    hidden = pk_ref.shape[1]
    odd = is_odd()
    cross, inner = cross_ref[...], inner_ref[...]
    halo = jnp.concatenate(
        [jnp.where(odd, inner, cross), jnp.where(odd, cross, inner)], axis=0
    ).astype(F32)
    low = normalize_rows(halo)[0].astype(BF16)
    first = first_half((128, 128))
    for c in range(0, 2 * hidden, 256):
        outer = dot(low, w_ref[:, hidden + c : hidden + c + 256]).astype(BF16).astype(F32)
        for j in (0, 128):
            at = c + j
            ext_ref[0:ROW, :] = outer[:ROW, j : j + 128]
            ext_ref[ROW : ROW + 128, :] = proj_ref[:, hidden + at : hidden + at + 128].astype(F32)
            ext_ref[ROW + 128 :, :] = outer[ROW:, j : j + 128]
            pooled = pool_lanes(ext_ref, load_taps(kern_ref, slice(at, at + 128)), False, (0, 1, 2, 3)).astype(BF16)
            if at < hidden:
                pk_ref[:, at : at + 128] = pooled
                kv_ref[:, at : at + 128] = pair_unit(pooled.astype(F32), first)[0].astype(BF16)
            else:
                kv_ref[:, at : at + 128] = pooled


def attention_kernel(
    layout, owner_ref, tau_ref, proj_ref, own_ref, cross_ref, inner_ref, grad_ref,
    att_ref, gq_ref, part_own_ref, part_near_ref,
):
    hidden = att_ref.shape[1]
    tile = this_tile(layout)
    from_cross = lists(owner_ref, tile, tile - 1) ^ is_odd()
    first = first_half((128, 128))
    first_low = first_half((256, 128))

    def both(at):
        near = jnp.where(from_cross, cross_ref[:, at : at + PW], inner_ref[:, at : at + PW])
        return jnp.concatenate([own_ref[:, at : at + PW], near], axis=0)

    def masked(rows):
        zero = jnp.zeros_like(rows)
        return jnp.concatenate(
            [jnp.where(first_low, rows, zero), jnp.where(first_low, zero, rows)], axis=0
        )

    for p in range(PAIRS):
        at = p * PW
        g2 = grad_ref[:, at : at + PW]
        q_unit, q_inverse = pair_unit(proj_ref[:, at : at + PW].astype(F32), first)
        q_low = q_unit.astype(BF16)
        keys = masked(both(at))
        values = masked(both(hidden + at))
        scores = dot_nt(keys, q_low)
        grad_probs = dot_nt(values, g2)
        probs, grads = [], []
        for half in range(2):
            scale = tau_ref[2 * p + half]
            cut = slice(half * 256, half * 256 + 256)
            exponent = jnp.exp(scores[cut] * scale)
            prob = exponent * (1.0 / jnp.sum(exponent, axis=0, keepdims=True))
            gp = grad_probs[cut]
            delta = jnp.sum(prob * gp, axis=0, keepdims=True)
            probs.append(prob.astype(BF16))
            grads.append((scale * prob * (gp - delta)).astype(BF16))
        prob_low = jnp.concatenate(probs, axis=0)
        grad_scores = jnp.concatenate(grads, axis=0)
        att_ref[:, at : at + PW] = dot(values.T, prob_low).T.astype(BF16)
        grad_q = dot(keys.T, grad_scores).T
        gq_ref[:, at : at + PW] = pair_unit_back(q_unit, q_inverse, grad_q, first).astype(BF16)
        grad_k = dot(grad_scores, q_low)
        grad_v = dot(prob_low, g2)
        grad_k = jnp.where(first_low, grad_k[:256], grad_k[256:]).astype(BF16)
        grad_v = jnp.where(first_low, grad_v[:256], grad_v[256:]).astype(BF16)
        part_own_ref[:, at : at + PW] = grad_k[:128]
        part_near_ref[:, at : at + PW] = grad_k[128:]
        part_own_ref[:, hidden + at : hidden + at + PW] = grad_v[:128]
        part_near_ref[:, hidden + at : hidden + at + PW] = grad_v[128:]


def attention_output_kernel(layout, *refs):
    ins, (wout_ref, b_ref), outs = refs[:7], refs[7:9], refs[9:13]
    out_ref, wout_buf, b_buf, sems = refs[13:]
    get_w = stream(wout_ref, wout_buf, sems.at[0], WHOLE)
    get_b = stream(b_ref, b_buf, sems.at[1], WHOLE)
    attention_kernel(layout, *ins, *outs)
    get_w(0)
    get_b(0)
    output_kernel(outs[0], wout_buf, b_buf, out_ref)


def settle_kernel(*refs):
    half = len(refs) // 2
    for source, target in zip(refs[:half], refs[half:]):
        target[...] = source[...]


def output_kernel(att_ref, wout_ref, b_ref, out_ref):
    att = att_ref[...]
    for c in range(0, out_ref.shape[1], 256):
        cut = slice(c, c + 256)
        out_ref[:, cut] = (b_ref[:, cut].astype(F32) - dot(att, wout_ref[:, cut])).astype(BF16)


def key_kernel(layout, owner_ref, own_ref, cross_ref, inner_ref, pk_ref, out_ref, cross_out_ref, inner_out_ref):
    hidden = pk_ref.shape[1]
    first = first_half((128, 128))
    odd = is_odd()
    tile = this_tile(layout)
    last = TILES - 1
    use_prev = (tile > 0) & lists(owner_ref, jnp.maximum(tile - 1, 0), tile)
    use_next = (tile < last) & lists(owner_ref, jnp.minimum(tile + 1, last), tile)
    use_cross = (odd & use_next) | (~odd & use_prev)
    use_inner = (odd & use_prev) | (~odd & use_next)
    for at in range(0, 2 * hidden, 128):
        cut = slice(at, at + 128)
        total = own_ref[:, cut].astype(F32)
        total = total + jnp.where(use_cross, cross_ref[:, cut].astype(F32), 0.0)
        total = total + jnp.where(use_inner, inner_ref[:, cut].astype(F32), 0.0)
        if at < hidden:
            unit, inverse = pair_unit(pk_ref[:, cut].astype(F32), first)
            total = pair_unit_back(unit, inverse, total, first)
        total = total.astype(BF16)
        out_ref[:, cut] = total
        cross_out_ref[:, cut] = jnp.where(odd, total[ROW:], total[:ROW])
        inner_out_ref[:, cut] = jnp.where(odd, total[:ROW], total[ROW:])


def local_kernel(own_ref, gq_ref, w_ref, kern_ref, part_ref, acc_ref, ext_ref):
    hidden = gq_ref.shape[1]
    gq = gq_ref[...]
    for at in range(0, 2 * hidden, 128):
        cut = slice(at, at + 128)
        ext_ref[ROW : ROW + 128, :] = own_ref[:, cut].astype(F32)
        part_ref[:, cut] = pool_lanes(ext_ref, load_taps(kern_ref, cut), True, (1, 2))
        acc_ref[:, cut] = dot_nt(gq, w_ref[cut, :hidden])


def final_kernel(
    cross_ref, inner_ref, part_ref, acc_ref, w_ref, kern_ref, a_ref, ga_ref,
    out_ref, ext_ref, gp_ref, sum_ref,
):
    odd = is_odd()
    channels = part_ref.shape[1]
    hidden = channels // 2
    width = a_ref.shape[1]
    for at in range(0, channels, 128):
        cut = slice(at, at + 128)
        cross, inner = cross_ref[:, cut], inner_ref[:, cut]
        ext_ref[0:ROW, :] = jnp.where(odd, inner, cross).astype(F32)
        ext_ref[ROW + 128 :, :] = jnp.where(odd, cross, inner).astype(F32)
        pooled = pool_lanes(ext_ref, load_taps(kern_ref, cut), True, (0, 3))
        gp_ref[:, cut] = (part_ref[:, cut] + pooled).astype(BF16)
    grad_raw = gp_ref[...]
    for c in range(0, width, 256):
        cut = slice(c, c + 256)
        sum_ref[:, cut] = acc_ref[:, cut] + dot_nt(grad_raw, w_ref[cut, hidden:])
    normalized, inverse = normalize_rows(a_ref[...].astype(F32))
    grad = sum_ref[...]
    grad_mean = jnp.mean(grad, axis=-1, keepdims=True)
    cross_mean = jnp.mean(grad * normalized, axis=-1, keepdims=True)
    back = inverse * (grad - grad_mean - normalized * cross_mean)
    out_ref[...] = (ga_ref[...].astype(F32) + back).astype(BF16)


def grad_kernel(gb_ref, wout_ref, out_ref):
    gb = gb_ref[...]
    for c in range(0, out_ref.shape[1], 256):
        out_ref[:, c : c + 256] = dot_nt(gb, wout_ref[c : c + 256, :]).astype(BF16)


def call(kernel, name, outs, specs, flops, scratch=(), kind=BF16, limit=6):
    def run(*args):
        moved = sum(x.size * x.dtype.itemsize for x in args)
        args = [
            pltpu.with_memory_space_constraint(x, HBM) if space == HBM else x
            for x, space in zip(args, specs)
        ]
        return pl.pallas_call(
            kernel,
            name=name,
            out_shape=[jax.ShapeDtypeStruct(s, kind) for s in outs],
            in_specs=[pl.BlockSpec(memory_space=s) for s in specs],
            out_specs=[pl.BlockSpec(memory_space=VMEM) for _ in outs],
            scratch_shapes=list(scratch),
            compiler_params=pltpu.CompilerParams(vmem_limit_bytes=limit * 1024 * 1024),
            cost_estimate=pl.CostEstimate(flops=flops, bytes_accessed=moved, transcendentals=0),
        )(*args)

    return run


SECTIONS = 16
TILES = 16


def start_layout(section, x):
    return 0


def first_layout(section, x):
    return 0


def second_layout(section, x):
    return ((section & 7) + 1) >> 3


def place(layout, section, tile):
    return section * TILES + (tile ^ (2 * layout(section, tile // 4)))


AXES = ("section", "space")


def move(value, source, target, by):
    pairs = [
        (place(source, s, t), place(target, (s + by) % SECTIONS, t))
        for s in range(SECTIONS)
        for t in range(TILES)
    ]
    return lax.ppermute(value, AXES, pairs)


def swap_cross(value, source, target):
    pairs = []
    for s in range(SECTIONS):
        for t in range(1, TILES - 1, 2):
            pairs.append((place(source, s, t), place(target, s, t + 1)))
            pairs.append((place(source, s, t + 1), place(target, s, t)))
    return lax.ppermute(value, AXES, pairs)


def swap_inner(value, source, target):
    pairs = [(place(source, s, t), place(target, s, t ^ 1)) for s in range(SECTIONS) for t in range(TILES)]
    return lax.ppermute(value, AXES, pairs)


def exchange(cross, inner, source, target=None):
    target = target or source
    inner = swap_inner(inner, source, target)
    return swap_cross(cross, source, target), inner


def together(*values):
    return lax.optimization_barrier(values)


def edges(value):
    odd = lax.rem(lax.axis_index("space"), 2)
    cross = lax.dynamic_slice_in_dim(value, odd * ROW, ROW, 0)
    inner = lax.dynamic_slice_in_dim(value, (1 - odd) * ROW, ROW, 0)
    return cross, inner


def forward_project(a, w_qkv, halo):
    cross, inner = halo
    block, width = a.shape
    (proj,) = call(
        project_kernel, "project", [(block, w_qkv.shape[1])], [VMEM] * 2, 2 * block * width * w_qkv.shape[1]
    )(a, w_qkv)
    return proj, cross, inner


def first_project(a, w_qkv):
    block, width = a.shape
    columns = w_qkv.shape[1]
    return call(
        first_project_kernel, "firstproject", [(block, columns)], [HBM] * 2, 2 * block * width * columns,
        [VMEM(a.shape, BF16), VMEM(w_qkv.shape, BF16), VMEM((block, columns), F32), DMA((1,)), DMA((width // 256,))],
        limit=14,
    )(a, w_qkv)[0]


def forward_pool(proj, cross, inner, w_qkv, kern):
    block = proj.shape[0]
    hidden = proj.shape[1] // 3
    return call(
        pool_kernel, "pool", [(block, 2 * hidden), (block, hidden)], [VMEM] * 5,
        2 * block * w_qkv.shape[0] * 2 * hidden, [VMEM((256, 128), F32)],
    )(cross, inner, w_qkv, proj, kern)


def grad_attended(gb, w_out):
    block, width = gb.shape
    hidden = w_out.shape[0]
    return call(
        grad_kernel, "gradatt", [(block, hidden)], [VMEM] * 2, 2 * block * width * hidden
    )(gb, w_out)[0]


def attend(layout, owner, tau, proj, kv, cross, inner, grad):
    block, hidden = grad.shape
    return call(
        functools.partial(attention_kernel, layout), "attention",
        [(block, hidden), (block, hidden), (block, 2 * hidden), (block, 2 * hidden)],
        [SMEM] * 2 + [VMEM] * 5, 2 * block * 512 * hidden * 8,
    )(owner, tau, proj, kv, cross, inner, grad)


def attend_rebuild(layout, owner, tau, proj, kv, cross, inner, grad, w_out, b):
    block, hidden = grad.shape
    return call(
        functools.partial(attention_output_kernel, layout), "attendout",
        [(block, hidden), (block, hidden), (block, 2 * hidden), (block, 2 * hidden), b.shape],
        [SMEM] * 2 + [VMEM] * 5 + [HBM] * 2, 2 * block * 512 * hidden * 8,
        [VMEM(w_out.shape, BF16), VMEM(b.shape, BF16), DMA((2, 1))],
        limit=9,
    )(owner, tau, proj, kv, cross, inner, grad, w_out, b)


def settle(*values):
    return call(settle_kernel, "settle", [v.shape for v in values], [VMEM] * len(values), 1)(*values)


def rebuild(att, w_out, b):
    block, width = b.shape
    return call(
        output_kernel, "output", [(block, width)], [VMEM] * 3, 2 * block * width * w_out.shape[0]
    )(att, w_out, b)[0]


def key_sums(layout, owner, own, cross, inner, pk):
    block, channels = own.shape
    return call(
        functools.partial(key_kernel, layout), "keys",
        [(block, channels), (ROW, channels), (ROW, channels)],
        [SMEM] + [VMEM] * 4, block * channels * 40,
    )(owner, own, cross, inner, pk)


def finish_local(gpool, gq, w_qkv, kern):
    block, channels = gpool.shape
    width = w_qkv.shape[0]
    return call(
        local_kernel, "local", [(block, channels), (block, width)], [VMEM] * 4,
        2 * block * width * gq.shape[1], [VMEM((256, 128), F32)], F32,
    )(gpool, gq, w_qkv, kern)


def finish(cross, inner, part, acc, w_qkv, kern, a, ga):
    block, width = a.shape
    channels = part.shape[1]
    return call(
        final_kernel, "final", [(block, width)], [VMEM] * 8, 2 * block * width * channels,
        [
            VMEM((256, 128), F32),
            VMEM((block, channels), BF16),
            VMEM((block, width), F32),
        ],
    )(cross, inner, part, acc, w_qkv, kern, a, ga)[0]


def body(top_a, top_b, grad_a, grad_b, w_qkv, w_out, kernel, tau, owner):
    a, b, ga, gb = top_a[0], top_b[0], grad_a[0], grad_b[0]
    w_qkv, w_out, tau = w_qkv[0], w_out[0], tau[0]
    kern = jnp.transpose(kernel, (1, 0, 2))
    one, two, start = first_layout, second_layout, start_layout

    halo = exchange(*edges(a), start, one)
    b2 = move(a, one, two, -1)
    ga2 = move(gb, one, two, -1)
    proj1 = first_project(a, w_qkv)
    cross, inner = halo
    kv1, pk1 = forward_pool(proj1, cross, inner, w_qkv, kern)
    cross, inner = exchange(kv1, kv1, one)
    grad1 = grad_attended(gb, w_out)
    cross, inner, b2, ga2, grad1 = together(cross, inner, b2, ga2, grad1)
    _, gq1, own1, near1, rebuilt1 = attend_rebuild(
        one, owner, tau, proj1, kv1, cross, inner, grad1, w_out, b
    )
    cross, inner = exchange(near1, near1, one)
    a2 = move(rebuilt1, one, two, -1)
    gpool1, cross, inner = key_sums(one, owner, own1, cross, inner, pk1)
    cross, inner = exchange(cross, inner, one)
    part1, acc1 = finish_local(gpool1, gq1, w_qkv, kern)
    new_grad1 = finish(cross, inner, part1, acc1, w_qkv, kern, a, ga)

    proj2, cross, inner = forward_project(a2, w_qkv, exchange(*edges(a2), two))
    kv2, pk2 = forward_pool(proj2, cross, inner, w_qkv, kern)
    kv2, new_grad1 = together(kv2, new_grad1)
    gb2 = move(new_grad1, one, two, -1)
    cross, inner = exchange(kv2, kv2, two)
    grad2 = grad_attended(gb2, w_out)
    passed_a = move(gb2, two, start, -1)
    att2, gq2, own2, near2 = attend(two, owner, tau, proj2, kv2, cross, inner, grad2)
    cross, inner = exchange(near2, near2, two)
    att2, passed_a = together(att2, passed_a)
    rebuilt2 = rebuild(att2, w_out, b2)
    cross, inner, rebuilt2, late = together(cross, inner, rebuilt2, a2)
    rebuilt_b = move(late, two, start, -1)
    gpool2, cross, inner = key_sums(two, owner, own2, cross, inner, pk2)
    cross, inner = exchange(cross, inner, two)
    part2, acc2 = finish_local(gpool2, gq2, w_qkv, kern)
    cross, inner, rebuilt2, rebuilt_b = together(cross, inner, rebuilt2, rebuilt_b)
    rebuilt_a = move(rebuilt2, two, start, -1)
    new_grad2 = finish(cross, inner, part2, acc2, w_qkv, kern, a2, ga2)
    passed_b = move(new_grad2, two, start, -1)
    rebuilt_a, rebuilt_b, passed_a = settle(rebuilt_a, rebuilt_b, passed_a)
    return rebuilt_a[None], rebuilt_b[None], passed_a[None], passed_b[None]


def solution(mesh):
    state = P("section", "space", None)
    weights = P("section", None, None)
    return jax.shard_map(
        body,
        mesh=mesh,
        in_specs=(state,) * 4 + (weights,) * 3 + (P("section", None), P()),
        out_specs=(state,) * 4,
        check_vma=False,
    )
```

```python
import functools

import jax
import jax.numpy as jnp
from jax import lax
from jax.experimental import pallas as pl
from jax.experimental.pallas import tpu as pltpu
from jax.sharding import PartitionSpec as P

HEADS = 12
HEAD = 64
FT = 4
FW = 16
PAIRS = HEADS // 2
PW = 2 * HEAD
ROW = FT * FW

EPS_NORM = 1e-05
EPS_HEAD = 1e-06

F32 = jnp.float32
BF16 = jnp.bfloat16
VMEM = pltpu.VMEM
SMEM = pltpu.SMEM
HBM = pltpu.HBM
DMA = pltpu.SemaphoreType.DMA


def dot(a, b):
    return jnp.dot(a, b, preferred_element_type=F32)


def dot_nt(a, b):
    return lax.dot_general(a, b, (((1,), (1,)), ((), ())), preferred_element_type=F32)


def normalize_rows(features):
    average = jnp.mean(features, axis=-1, keepdims=True)
    centred = features - average
    inverse = lax.rsqrt(jnp.mean(centred * centred, axis=-1, keepdims=True) + EPS_NORM)
    return centred * inverse, inverse


def first_half(shape):
    return lax.broadcasted_iota(jnp.int32, shape, 1) < HEAD


def pair_sums(values, first):
    low = jnp.sum(jnp.where(first, values, 0.0), axis=-1, keepdims=True)
    high = jnp.sum(jnp.where(first, 0.0, values), axis=-1, keepdims=True)
    return jnp.where(first, low, high)


def pair_unit(values, first):
    inverse = lax.rsqrt(pair_sums(values * values, first) + EPS_HEAD)
    return values * inverse, inverse


def pair_unit_back(unit, inverse, gradient, first):
    return inverse * (gradient - unit * pair_sums(unit * gradient, first))


def pool_lanes(ext_ref, taps, flip, rows):
    column = lax.broadcasted_iota(jnp.int32, (FW, 128), 0)
    blocks = []
    for row in range(2):
        for frame in range(FT):
            parts = [None, None, None]
            for dr in range(3):
                if row + dr not in rows:
                    continue
                for df in range(3):
                    source = frame + df - 1
                    if source < 0 or source >= FT:
                        continue
                    start = (row + dr) * ROW + source * FW
                    block = ext_ref[start : start + FW, :]
                    for dc in range(3):
                        tap = dr * 9 + df * 3 + dc
                        term = taps[26 - tap if flip else tap] * block
                        parts[dc] = term if parts[dc] is None else parts[dc] + term
            left = jnp.where(column == 0, 0.0, pltpu.roll(parts[0], 1, 0))
            right = jnp.where(column == FW - 1, 0.0, pltpu.roll(parts[2], FW - 1, 0))
            blocks.append(parts[1] + left + right)
    return jnp.concatenate(blocks, axis=0)


def load_taps(kern_ref, lanes):
    return [jnp.broadcast_to(kern_ref[t, :, lanes], (FW, 128)) for t in range(27)]


def is_odd():
    return (lax.axis_index("space") & 1) == 1


def lists(owner_ref, row, tile):
    return (owner_ref[row, 0] == tile) | (owner_ref[row, 1] == tile)


def this_tile(layout):
    space = lax.axis_index("space")
    return space ^ (2 * layout(lax.axis_index("section"), space >> 2))


def stream(ref, buf, sems, cuts):
    copies = [pltpu.make_async_copy(ref.at[cut], buf.at[cut], sems.at[k]) for k, cut in enumerate(cuts)]
    for copy in copies:
        copy.start()

    def get(k):
        copies[k].wait()
        return buf[cuts[k]]

    return get


WHOLE = [(slice(None), slice(None))]


def put_projected(q_ref, raw_ref, c, value):
    hidden = q_ref.shape[1]
    if c < hidden:
        q_ref[:, c : c + 256] = value.astype(BF16)
    else:
        raw_ref[:, c - hidden : c - hidden + 256] = value.astype(BF16)


def project_kernel(a_ref, w_ref, q_ref, raw_ref):
    low = normalize_rows(a_ref[...].astype(F32))[0].astype(BF16)
    for c in range(0, w_ref.shape[1], 256):
        put_projected(q_ref, raw_ref, c, dot(low, w_ref[:, c : c + 256]))


def first_project_kernel(a_ref, w_ref, q_ref, raw_ref, a_buf, w_buf, acc_ref, sems, w_sems):
    get_a = stream(a_ref, a_buf, sems, WHOLE)
    cuts = [(slice(r, r + 256), slice(None)) for r in range(0, w_ref.shape[0], 256)]
    get = stream(w_ref, w_buf, w_sems, cuts)
    low = normalize_rows(get_a(0).astype(F32))[0].astype(BF16)
    for k, (rows, _) in enumerate(cuts):
        piece = get(k)
        for c in range(0, w_ref.shape[1], 256):
            cut = slice(c, c + 256)
            total = dot(low[:, rows], piece[:, cut])
            if k:
                total = total + acc_ref[:, cut]
            if k + 1 < len(cuts):
                acc_ref[:, cut] = total
            else:
                put_projected(q_ref, raw_ref, c, total)


def pool_kernel(cross_ref, inner_ref, w_ref, raw_ref, kern_ref, kv_ref, pk_ref, ext_ref):
    hidden = pk_ref.shape[1]
    odd = is_odd()
    cross, inner = cross_ref[...], inner_ref[...]
    halo = jnp.concatenate(
        [jnp.where(odd, inner, cross), jnp.where(odd, cross, inner)], axis=0
    ).astype(F32)
    low = normalize_rows(halo)[0].astype(BF16)
    first = first_half((128, 128))
    for c in range(0, 2 * hidden, 256):
        outer = dot(low, w_ref[:, hidden + c : hidden + c + 256]).astype(BF16).astype(F32)
        for j in (0, 128):
            at = c + j
            ext_ref[0:ROW, :] = outer[:ROW, j : j + 128]
            ext_ref[ROW : ROW + 128, :] = raw_ref[:, at : at + 128].astype(F32)
            ext_ref[ROW + 128 :, :] = outer[ROW:, j : j + 128]
            pooled = pool_lanes(ext_ref, load_taps(kern_ref, slice(at, at + 128)), False, (0, 1, 2, 3)).astype(BF16)
            if at < hidden:
                pk_ref[:, at : at + 128] = pooled
                kv_ref[:, at : at + 128] = pair_unit(pooled.astype(F32), first)[0].astype(BF16)
            else:
                kv_ref[:, at : at + 128] = pooled


def attention_kernel(
    layout, owner_ref, tau_ref, proj_ref, own_ref, cross_ref, inner_ref, grad_ref,
    att_ref, gq_ref, part_own_ref, part_near_ref,
):
    hidden = att_ref.shape[1]
    tile = this_tile(layout)
    from_cross = lists(owner_ref, tile, tile - 1) ^ is_odd()
    first = first_half((128, 128))
    first_low = first_half((256, 128))

    def both(at):
        near = jnp.where(from_cross, cross_ref[:, at : at + PW], inner_ref[:, at : at + PW])
        return jnp.concatenate([own_ref[:, at : at + PW], near], axis=0)

    def masked(rows):
        zero = jnp.zeros_like(rows)
        return jnp.concatenate(
            [jnp.where(first_low, rows, zero), jnp.where(first_low, zero, rows)], axis=0
        )

    for p in range(PAIRS):
        at = p * PW
        g2 = grad_ref[:, at : at + PW]
        q_unit, q_inverse = pair_unit(proj_ref[:, at : at + PW].astype(F32), first)
        q_low = q_unit.astype(BF16)
        keys = masked(both(at))
        values = masked(both(hidden + at))
        scores = dot_nt(keys, q_low)
        grad_probs = dot_nt(values, g2)
        probs, grads = [], []
        for half in range(2):
            scale = tau_ref[2 * p + half]
            cut = slice(half * 256, half * 256 + 256)
            exponent = jnp.exp(scores[cut] * scale)
            prob = exponent * (1.0 / jnp.sum(exponent, axis=0, keepdims=True))
            gp = grad_probs[cut]
            delta = jnp.sum(prob * gp, axis=0, keepdims=True)
            probs.append(prob.astype(BF16))
            grads.append((scale * prob * (gp - delta)).astype(BF16))
        prob_low = jnp.concatenate(probs, axis=0)
        grad_scores = jnp.concatenate(grads, axis=0)
        att_ref[:, at : at + PW] = dot(values.T, prob_low).T.astype(BF16)
        grad_q = dot(keys.T, grad_scores).T
        gq_ref[:, at : at + PW] = pair_unit_back(q_unit, q_inverse, grad_q, first).astype(BF16)
        grad_k = dot(grad_scores, q_low)
        grad_v = dot(prob_low, g2)
        grad_k = jnp.where(first_low, grad_k[:256], grad_k[256:]).astype(BF16)
        grad_v = jnp.where(first_low, grad_v[:256], grad_v[256:]).astype(BF16)
        part_own_ref[:, at : at + PW] = grad_k[:128]
        part_near_ref[:, at : at + PW] = grad_k[128:]
        part_own_ref[:, hidden + at : hidden + at + PW] = grad_v[:128]
        part_near_ref[:, hidden + at : hidden + at + PW] = grad_v[128:]


def attention_output_kernel(layout, *refs):
    ins, (wout_ref, b_ref), outs = refs[:7], refs[7:9], refs[9:13]
    out_ref, wout_buf, b_buf, sems = refs[13:]
    get_w = stream(wout_ref, wout_buf, sems.at[0], WHOLE)
    get_b = stream(b_ref, b_buf, sems.at[1], WHOLE)
    attention_kernel(layout, *ins, *outs)
    get_w(0)
    get_b(0)
    output_kernel(outs[0], wout_buf, b_buf, out_ref)


def settle_kernel(*refs):
    half = len(refs) // 2
    for source, target in zip(refs[:half], refs[half:]):
        target[...] = source[...]


def output_kernel(att_ref, wout_ref, b_ref, out_ref):
    att = att_ref[...]
    for c in range(0, out_ref.shape[1], 256):
        cut = slice(c, c + 256)
        out_ref[:, cut] = (b_ref[:, cut].astype(F32) - dot(att, wout_ref[:, cut])).astype(BF16)


def key_kernel(layout, owner_ref, own_ref, cross_ref, inner_ref, pk_ref, out_ref, cross_out_ref, inner_out_ref):
    hidden = pk_ref.shape[1]
    first = first_half((128, 128))
    odd = is_odd()
    tile = this_tile(layout)
    last = TILES - 1
    use_prev = (tile > 0) & lists(owner_ref, jnp.maximum(tile - 1, 0), tile)
    use_next = (tile < last) & lists(owner_ref, jnp.minimum(tile + 1, last), tile)
    use_cross = (odd & use_next) | (~odd & use_prev)
    use_inner = (odd & use_prev) | (~odd & use_next)
    for at in range(0, 2 * hidden, 128):
        cut = slice(at, at + 128)
        total = own_ref[:, cut].astype(F32)
        total = total + jnp.where(use_cross, cross_ref[:, cut].astype(F32), 0.0)
        total = total + jnp.where(use_inner, inner_ref[:, cut].astype(F32), 0.0)
        if at < hidden:
            unit, inverse = pair_unit(pk_ref[:, cut].astype(F32), first)
            total = pair_unit_back(unit, inverse, total, first)
        total = total.astype(BF16)
        out_ref[:, cut] = total
        cross_out_ref[:, cut] = jnp.where(odd, total[ROW:], total[:ROW])
        inner_out_ref[:, cut] = jnp.where(odd, total[:ROW], total[ROW:])


def local_kernel(own_ref, gq_ref, w_ref, kern_ref, part_ref, acc_ref, ext_ref):
    hidden = gq_ref.shape[1]
    gq = gq_ref[...]
    for at in range(0, 2 * hidden, 128):
        cut = slice(at, at + 128)
        ext_ref[ROW : ROW + 128, :] = own_ref[:, cut].astype(F32)
        part_ref[:, cut] = pool_lanes(ext_ref, load_taps(kern_ref, cut), True, (1, 2))
        acc_ref[:, cut] = dot_nt(gq, w_ref[cut, :hidden])


def final_kernel(
    cross_ref, inner_ref, part_ref, acc_ref, w_ref, kern_ref, a_ref, ga_ref,
    out_ref, ext_ref, gp_ref, sum_ref,
):
    odd = is_odd()
    channels = part_ref.shape[1]
    hidden = channels // 2
    width = a_ref.shape[1]
    for at in range(0, channels, 128):
        cut = slice(at, at + 128)
        cross, inner = cross_ref[:, cut], inner_ref[:, cut]
        ext_ref[0:ROW, :] = jnp.where(odd, inner, cross).astype(F32)
        ext_ref[ROW + 128 :, :] = jnp.where(odd, cross, inner).astype(F32)
        pooled = pool_lanes(ext_ref, load_taps(kern_ref, cut), True, (0, 3))
        gp_ref[:, cut] = (part_ref[:, cut] + pooled).astype(BF16)
    grad_raw = gp_ref[...]
    for c in range(0, width, 256):
        cut = slice(c, c + 256)
        sum_ref[:, cut] = acc_ref[:, cut] + dot_nt(grad_raw, w_ref[cut, hidden:])
    normalized, inverse = normalize_rows(a_ref[...].astype(F32))
    grad = sum_ref[...]
    grad_mean = jnp.mean(grad, axis=-1, keepdims=True)
    cross_mean = jnp.mean(grad * normalized, axis=-1, keepdims=True)
    back = inverse * (grad - grad_mean - normalized * cross_mean)
    out_ref[...] = (ga_ref[...].astype(F32) + back).astype(BF16)


def grad_kernel(gb_ref, wout_ref, out_ref):
    gb = gb_ref[...]
    for c in range(0, out_ref.shape[1], 256):
        out_ref[:, c : c + 256] = dot_nt(gb, wout_ref[c : c + 256, :]).astype(BF16)


def call(kernel, name, outs, specs, flops, scratch=(), kind=BF16, limit=6):
    def run(*args):
        moved = sum(x.size * x.dtype.itemsize for x in args)
        args = [
            pltpu.with_memory_space_constraint(x, HBM) if space == HBM else x
            for x, space in zip(args, specs)
        ]
        return pl.pallas_call(
            kernel,
            name=name,
            out_shape=[jax.ShapeDtypeStruct(s, kind) for s in outs],
            in_specs=[pl.BlockSpec(memory_space=s) for s in specs],
            out_specs=[pl.BlockSpec(memory_space=VMEM) for _ in outs],
            scratch_shapes=list(scratch),
            compiler_params=pltpu.CompilerParams(vmem_limit_bytes=limit * 1024 * 1024),
            cost_estimate=pl.CostEstimate(flops=flops, bytes_accessed=moved, transcendentals=0),
        )(*args)

    return run


SECTIONS = 16
TILES = 16


def start_layout(section, x):
    return 0


def first_layout(section, x):
    return 0


def second_layout(section, x):
    return ((section & 7) + 1) >> 3


def place(layout, section, tile):
    return section * TILES + (tile ^ (2 * layout(section, tile // 4)))


AXES = ("section", "space")


def move(value, source, target, by):
    pairs = [
        (place(source, s, t), place(target, (s + by) % SECTIONS, t))
        for s in range(SECTIONS)
        for t in range(TILES)
    ]
    return lax.ppermute(value, AXES, pairs)


def swap_cross(value, source, target):
    pairs = []
    for s in range(SECTIONS):
        for t in range(1, TILES - 1, 2):
            pairs.append((place(source, s, t), place(target, s, t + 1)))
            pairs.append((place(source, s, t + 1), place(target, s, t)))
    return lax.ppermute(value, AXES, pairs)


def swap_inner(value, source, target):
    pairs = [(place(source, s, t), place(target, s, t ^ 1)) for s in range(SECTIONS) for t in range(TILES)]
    return lax.ppermute(value, AXES, pairs)


def exchange(cross, inner, source, target=None):
    target = target or source
    inner = swap_inner(inner, source, target)
    return swap_cross(cross, source, target), inner


def together(*values):
    return lax.optimization_barrier(values)


def edges(value):
    odd = lax.rem(lax.axis_index("space"), 2)
    cross = lax.dynamic_slice_in_dim(value, odd * ROW, ROW, 0)
    inner = lax.dynamic_slice_in_dim(value, (1 - odd) * ROW, ROW, 0)
    return cross, inner


def forward_project(a, w_qkv):
    block, width = a.shape
    columns = w_qkv.shape[1]
    return call(
        project_kernel, "project", [(block, columns // 3), (block, columns // 3 * 2)], [VMEM] * 2,
        2 * block * width * columns,
    )(a, w_qkv)


def first_project(a, w_qkv):
    block, width = a.shape
    columns = w_qkv.shape[1]
    return call(
        first_project_kernel, "firstproject", [(block, columns // 3), (block, columns // 3 * 2)], [HBM] * 2, 2 * block * width * columns,
        [VMEM(a.shape, BF16), VMEM(w_qkv.shape, BF16), VMEM((block, columns), F32), DMA((1,)), DMA((width // 256,))],
        limit=14,
    )(a, w_qkv)


def forward_pool(raw, cross, inner, w_qkv, kern):
    block, channels = raw.shape
    hidden = channels // 2
    return call(
        pool_kernel, "pool", [(block, 2 * hidden), (block, hidden)], [VMEM] * 5,
        2 * block * w_qkv.shape[0] * 2 * hidden, [VMEM((256, 128), F32)],
    )(cross, inner, w_qkv, raw, kern)


def grad_attended(gb, w_out):
    block, width = gb.shape
    hidden = w_out.shape[0]
    return call(
        grad_kernel, "gradatt", [(block, hidden)], [VMEM] * 2, 2 * block * width * hidden
    )(gb, w_out)[0]


def attend(layout, owner, tau, proj, kv, cross, inner, grad):
    block, hidden = grad.shape
    return call(
        functools.partial(attention_kernel, layout), "attention",
        [(block, hidden), (block, hidden), (block, 2 * hidden), (block, 2 * hidden)],
        [SMEM] * 2 + [VMEM] * 5, 2 * block * 512 * hidden * 8,
    )(owner, tau, proj, kv, cross, inner, grad)


def attend_rebuild(layout, owner, tau, proj, kv, cross, inner, grad, w_out, b):
    block, hidden = grad.shape
    return call(
        functools.partial(attention_output_kernel, layout), "attendout",
        [(block, hidden), (block, hidden), (block, 2 * hidden), (block, 2 * hidden), b.shape],
        [SMEM] * 2 + [VMEM] * 5 + [HBM] * 2, 2 * block * 512 * hidden * 8,
        [VMEM(w_out.shape, BF16), VMEM(b.shape, BF16), DMA((2, 1))],
        limit=9,
    )(owner, tau, proj, kv, cross, inner, grad, w_out, b)


def settle(*values):
    return call(settle_kernel, "settle", [v.shape for v in values], [VMEM] * len(values), 1)(*values)


def rebuild(att, w_out, b):
    block, width = b.shape
    return call(
        output_kernel, "output", [(block, width)], [VMEM] * 3, 2 * block * width * w_out.shape[0]
    )(att, w_out, b)[0]


def key_sums(layout, owner, own, cross, inner, pk):
    block, channels = own.shape
    return call(
        functools.partial(key_kernel, layout), "keys",
        [(block, channels), (ROW, channels), (ROW, channels)],
        [SMEM] + [VMEM] * 4, block * channels * 40,
    )(owner, own, cross, inner, pk)


def finish_local(gpool, gq, w_qkv, kern):
    block, channels = gpool.shape
    width = w_qkv.shape[0]
    return call(
        local_kernel, "local", [(block, channels), (block, width)], [VMEM] * 4,
        2 * block * width * gq.shape[1], [VMEM((256, 128), F32)], F32,
    )(gpool, gq, w_qkv, kern)


def finish(cross, inner, part, acc, w_qkv, kern, a, ga):
    block, width = a.shape
    channels = part.shape[1]
    return call(
        final_kernel, "final", [(block, width)], [VMEM] * 8, 2 * block * width * channels,
        [
            VMEM((256, 128), F32),
            VMEM((block, channels), BF16),
            VMEM((block, width), F32),
        ],
    )(cross, inner, part, acc, w_qkv, kern, a, ga)[0]


def body(top_a, top_b, grad_a, grad_b, w_qkv, w_out, kernel, tau, owner):
    a, b, ga, gb = top_a[0], top_b[0], grad_a[0], grad_b[0]
    w_qkv, w_out, tau = w_qkv[0], w_out[0], tau[0]
    kern = jnp.transpose(kernel, (1, 0, 2))
    one, two, start = first_layout, second_layout, start_layout

    halo = exchange(*edges(a), start, one)
    b2 = move(a, one, two, -1)
    ga2 = move(gb, one, two, -1)
    q1, raw1 = first_project(a, w_qkv)
    cross, inner = halo
    kv1, pk1 = forward_pool(raw1, cross, inner, w_qkv, kern)
    cross, inner = exchange(kv1, kv1, one)
    grad1 = grad_attended(gb, w_out)
    cross, inner, b2, ga2, grad1 = together(cross, inner, b2, ga2, grad1)
    _, gq1, own1, near1, rebuilt1 = attend_rebuild(
        one, owner, tau, q1, kv1, cross, inner, grad1, w_out, b
    )
    cross, inner = exchange(near1, near1, one)
    a2 = move(rebuilt1, one, two, -1)
    gpool1, cross, inner = key_sums(one, owner, own1, cross, inner, pk1)
    cross, inner = exchange(cross, inner, one)
    part1, acc1 = finish_local(gpool1, gq1, w_qkv, kern)
    new_grad1 = finish(cross, inner, part1, acc1, w_qkv, kern, a, ga)

    cross, inner = exchange(*edges(a2), two)
    q2, raw2 = forward_project(a2, w_qkv)
    kv2, pk2 = forward_pool(raw2, cross, inner, w_qkv, kern)
    kv2, new_grad1 = together(kv2, new_grad1)
    gb2 = move(new_grad1, one, two, -1)
    cross, inner = exchange(kv2, kv2, two)
    grad2 = grad_attended(gb2, w_out)
    passed_a = move(gb2, two, start, -1)
    att2, gq2, own2, near2 = attend(two, owner, tau, q2, kv2, cross, inner, grad2)
    cross, inner = exchange(near2, near2, two)
    att2, passed_a = together(att2, passed_a)
    rebuilt2 = rebuild(att2, w_out, b2)
    cross, inner, rebuilt2, late = together(cross, inner, rebuilt2, a2)
    rebuilt_b = move(late, two, start, -1)
    gpool2, cross, inner = key_sums(two, owner, own2, cross, inner, pk2)
    cross, inner = exchange(cross, inner, two)
    part2, acc2 = finish_local(gpool2, gq2, w_qkv, kern)
    cross, inner, rebuilt2, rebuilt_b = together(cross, inner, rebuilt2, rebuilt_b)
    rebuilt_a = move(rebuilt2, two, start, -1)
    new_grad2 = finish(cross, inner, part2, acc2, w_qkv, kern, a2, ga2)
    passed_b = move(new_grad2, two, start, -1)
    rebuilt_a, rebuilt_b, passed_a = settle(rebuilt_a, rebuilt_b, passed_a)
    return rebuilt_a[None], rebuilt_b[None], passed_a[None], passed_b[None]


def solution(mesh):
    state = P("section", "space", None)
    weights = P("section", None, None)
    return jax.shard_map(
        body,
        mesh=mesh,
        in_specs=(state,) * 4 + (weights,) * 3 + (P("section", None), P()),
        out_specs=(state,) * 4,
        check_vma=False,
    )
```
